32 devices in a mesh: parts: 2 (over x), dp: 2 (over core), tensor: 8 (over z, y).
Axes of the slice: x: 2, y: 2, z: 4, core: 2. Of those that a mesh axis runs over, the one named last changes fastest.
Arguments:
- home_token_rows: bfloat16 [12288, 8192], P(('parts', 'dp'), 'tensor'), parts along dimension 0, may hold values from -6 to 6
- block_target_group: int32 [96], P(('parts', 'dp')), parts along dimension 0, may hold values from 0 to 1
- block_send_slot: int32 [96], P(('parts', 'dp')), parts along dimension 0, may hold values from 0 to 15, as said below
- block_adapter_job: int32 [96], P(('parts', 'dp')), parts along dimension 0, may hold values from 0 to 15
- key_weight_matrix: bfloat16 [8192, 1024], P('tensor'), may hold values from -0.0625 to 0.0625
- down_factors: bfloat16 [8192, 256], P('tensor'), may hold values from -0.0625 to 0.0625
- up_factors: bfloat16 [256, 1024], P(None, 'tensor'), may hold values from -1.5 to 1.5
- output_gradient: bfloat16 [16384, 1024], P(('parts', 'dp'), 'tensor'), parts along dimension 0, may hold values from -6 to 6
Outputs:
- output: bfloat16 [16384, 1024], P(('parts', 'dp'), 'tensor'), parts along dimension 0
- grad_home: bfloat16 [12288, 8192], P(('parts', 'dp'), 'tensor'), parts along dimension 0
- grad_a: float32 [8192, 512], P('tensor', ('parts', 'dp')), parts along dimension 1
- up_factor_gradient: float32 [512, 1024], P(('parts', 'dp'), 'tensor'), parts along dimension 0
The draws below stay inside these ranges and needn't reach their ends.
There are 2 independent parts, one for each index of `parts`. The reference program is written for one: setup_inputs(seed, part) draws one part's arguments, and reference() takes and returns one part's arrays. A program takes and returns all parts, laid end to end along the dimension named above; an argument that names none is the same for every part. Nothing has to cross between parts.
Inputs may be any that keep to these rules, and one draw needn't show every extreme that they name: `block_send_slot`: among the blocks of one home group with one compute group, slots are distinct and run from 0 without gaps; each home group sends exactly 16 blocks to one of the compute groups.
All inputs are finite; a program needn't handle non-finite values.
Results may differ from the reference program's by a relative error of at most 0.001.
Values may be sent and summed in bfloat16 or wider, within the bound.
No kernel may reach another device: no remote copies, remote signals or barrier semaphores. Data moves between devices by JAX's collectives and lax.ppermute only.
A program may use at most 192 MiB of HBM per device.

```python
import jax
import jax.numpy as jnp
from jax import lax

MODEL_WIDTH = 8192
ADAPTER_RANK = 16
ADAPTER_JOBS = 16
BLOCK_ROWS = 128
CAP = 16
KEY_FEATURES = 1024
HB = 24
HOME = 6144
COMP = 8192
N_DP = 2


def packing(key):
    dest_parts = []
    slot_parts = []
    for source in range(N_DP):
        subkey = jax.random.fold_in(key, 100 + source)
        first_key, order_key = jax.random.split(subkey)
        pick = jax.random.randint(first_key, (), 0, 2)
        first = jnp.where(pick == 0, CAP, HB - CAP).astype(jnp.int32)
        order = jax.random.permutation(order_key, HB)
        place = jnp.zeros((HB,), jnp.int32).at[order].set(jnp.arange(HB, dtype=jnp.int32))
        dest_parts.append((place >= first).astype(jnp.int32))
        slot_parts.append(jnp.where(place < first, place, place - first).astype(jnp.int32))
    return (jnp.concatenate(dest_parts), jnp.concatenate(slot_parts))


def draw_block_target_group(key, part):
    shared = packing(key)
    return shared[0]


def draw_block_send_slot(key, part):
    shared = packing(key)
    return shared[1]


def set_ends(result, own_key, smallest, high):
    dims = result.shape
    spot = [jax.random.randint(jax.random.fold_in(own_key, axis), (), 0, dims[axis]) for axis in range(len(dims))]
    result = result.at[tuple(spot)].set(smallest)
    longest = dims.index(max(dims))
    spot[longest] = (spot[longest] + 1) % dims[longest]
    return result.at[tuple(spot)].set(high)


def level_of(stream_key, extent, cuts, low, top_value):
    def one(position, parts):
        draws = jax.random.uniform(jax.random.fold_in(jax.random.fold_in(stream_key, 6), position), (parts,), jnp.float32, low / len(cuts), top_value / len(cuts))
        return jnp.repeat(jnp.exp(draws), extent[position] // parts).reshape((-1,) + (1,) * (len(extent) - position - 1))

    factor_of = one(*cuts[0])
    for cut in cuts[1:]:
        factor_of = factor_of * one(*cut)
    return factor_of


def normal_values(own_key, shape, spread, bound, pieces=(), held_as=jnp.bfloat16):
    entries = jax.random.normal(own_key, shape, jnp.float32) * spread
    if len(pieces) > 0:
        entries = level_of(own_key, shape, pieces, -0.22, 0.18) * entries
    return jnp.clip(entries, min=-bound, max=bound).astype(held_as)


def setup_inputs(seed: int = 0, part: int = 0) -> dict:
    key_list = jax.random.split(jax.random.key(seed), 9)
    part_keys = jax.random.split(jax.random.fold_in(key_list[8], part), 9)
    return {
        "home_token_rows": normal_values(part_keys[0], (HOME, MODEL_WIDTH), 1.0, 6.0, ((0, 2), (1, 8))),
        "block_target_group": draw_block_target_group(jax.random.fold_in(jax.random.fold_in(key_list[8], part), 71), part),
        "block_send_slot": draw_block_send_slot(jax.random.fold_in(jax.random.fold_in(key_list[8], part), 71), part),
        "block_adapter_job": set_ends(jax.random.randint(part_keys[3], (N_DP * HB,), 0, ADAPTER_JOBS), jax.random.fold_in(part_keys[3], 1), 0, ADAPTER_JOBS - 1).astype(jnp.int32),
        "key_weight_matrix": normal_values(key_list[4], (MODEL_WIDTH, KEY_FEATURES), MODEL_WIDTH ** -0.5, 0.0625, ((0, 8),)),
        "down_factors": normal_values(key_list[5], (MODEL_WIDTH, ADAPTER_JOBS * ADAPTER_RANK), MODEL_WIDTH ** -0.5, 0.0625, ((0, 8),)),
        "up_factors": normal_values(key_list[6], (ADAPTER_JOBS * ADAPTER_RANK, KEY_FEATURES), 0.25, 1.5, ((1, 8),)),
        "output_gradient": normal_values(part_keys[7], (COMP, KEY_FEATURES), 1.0, 6.0, ((0, 2), (1, 8))),
    }


adapter_scale = 2.0
highest_precision = lax.Precision.HIGHEST


def reference(home_token_rows, block_target_group, block_send_slot, block_adapter_job, key_weight_matrix, down_factors, up_factors, output_gradient):
    home_count = N_DP * HB
    gathered_blocks = N_DP * N_DP * CAP
    source = jnp.arange(home_count, dtype=jnp.int32) // HB
    target = (block_target_group * (N_DP * CAP) + source * CAP + block_send_slot).astype(jnp.int32)
    comp_rows = jnp.zeros((gathered_blocks, BLOCK_ROWS, MODEL_WIDTH), jnp.bfloat16).at[target].set(home_token_rows.reshape(home_count, BLOCK_ROWS, MODEL_WIDTH))
    compute_jobs = jnp.zeros((gathered_blocks,), jnp.int32).at[target].set(block_adapter_job)
    down_blocks = down_factors.reshape(MODEL_WIDTH, ADAPTER_JOBS, ADAPTER_RANK).transpose(1, 0, 2)[compute_jobs].astype(jnp.float32)
    up_blocks = up_factors.reshape(ADAPTER_JOBS, ADAPTER_RANK, KEY_FEATURES)[compute_jobs].astype(jnp.float32)
    rows_float = comp_rows.astype(jnp.float32)
    lowrank_sum = jnp.einsum("nbd,ndr->nbr", rows_float, down_blocks, precision=highest_precision)
    flat_rows = comp_rows.reshape(gathered_blocks * BLOCK_ROWS, MODEL_WIDTH)
    frozen_output = jnp.dot(flat_rows, key_weight_matrix, preferred_element_type=jnp.float32)
    adapter_index = jnp.einsum("nbr,nrk->nbk", lowrank_sum, up_blocks, precision=highest_precision)
    output = (frozen_output + adapter_scale * adapter_index.reshape(gathered_blocks * BLOCK_ROWS, KEY_FEATURES)).astype(jnp.bfloat16)
    gradient_blocks = output_gradient.reshape(gathered_blocks, BLOCK_ROWS, KEY_FEATURES).astype(jnp.float32)
    reduced_gradient = adapter_scale * jnp.einsum("szm,sfm->szf", gradient_blocks, up_blocks, precision=highest_precision)
    through_sum = jnp.dot(output_gradient, key_weight_matrix.T, preferred_element_type=jnp.float32)
    lowrank_back = jnp.einsum("nbr,ndr->nbd", reduced_gradient, down_blocks, precision=highest_precision)
    grad_rows = (through_sum + lowrank_back.reshape(gathered_blocks * BLOCK_ROWS, MODEL_WIDTH)).astype(jnp.bfloat16)
    grad_home = grad_rows.reshape(gathered_blocks, BLOCK_ROWS, MODEL_WIDTH)[target].reshape(home_count * BLOCK_ROWS, MODEL_WIDTH)
    job_indicator = (compute_jobs[:, None] == jnp.arange(ADAPTER_JOBS, dtype=jnp.int32)[None, :]).astype(jnp.float32)
    a_terms = jnp.einsum("nbd,nbr->ndr", rows_float, reduced_gradient, precision=highest_precision)
    grad_a = jnp.einsum("nj,ndr->djr", job_indicator, a_terms, precision=highest_precision).reshape(MODEL_WIDTH, ADAPTER_JOBS * ADAPTER_RANK)
    up_terms = jnp.einsum("nbr,nbk->nrk", lowrank_sum, gradient_blocks, precision=highest_precision)
    up_factor_gradient = adapter_scale * jnp.einsum("wq,wbz->qbz", job_indicator, up_terms, precision=highest_precision).reshape(ADAPTER_JOBS * ADAPTER_RANK, KEY_FEATURES)
    return (output, grad_home, grad_a, up_factor_gradient)
```

```python
import functools

import jax
import jax.numpy as jnp
from jax import lax
from jax.experimental import pallas as pl
from jax.experimental.pallas import tpu as pltpu
from jax.sharding import PartitionSpec as P

ADAPTER_RANK = 16
SCALE = 2.0


def split2(v):
    high = lax.reduce_precision(v, 8, 7)
    return high.astype(jnp.bfloat16), (v - high).astype(jnp.bfloat16)


def dot32(a, b, dims):
    return lax.dot_general(a, b, (dims, ((), ())), preferred_element_type=jnp.float32)


def general(x, group, slot, job, w, a, b, dy):
    groups = lax.axis_size("dp")
    blocks = group.shape[0]
    rows, features = x.shape
    length = rows // blocks
    columns = dy.shape[1]
    cap = dy.shape[0] // length // groups
    jobs = a.shape[1] // ADAPTER_RANK
    index = group * cap + slot
    got = lax.all_to_all(
        dy.reshape(groups, cap * length, columns), "dp", split_axis=0, concat_axis=0, tiled=True
    )
    dy_home = got.reshape(groups * cap, length, columns)[index].reshape(rows, columns)
    hot = jnp.repeat(job, length)[:, None] == (
        jnp.arange(jobs * ADAPTER_RANK, dtype=jnp.int32) // ADAPTER_RANK
    )

    def of_job(terms):
        kept = jnp.where(hot, terms, 0.0).reshape(rows, jobs, ADAPTER_RANK)
        return jnp.sum(kept, axis=1).T

    def spread(sums):
        return jnp.where(hot, jnp.tile(sums.T, (1, jobs)), 0.0)

    parts = jnp.stack(
        (of_job(dot32(x, a, ((1,), (0,)))), of_job(SCALE * dot32(dy_home, b, ((1,), (1,)))))
    )
    sums = lax.psum(parts, "tensor")
    low, low_grad = spread(sums[0]), spread(sums[1])
    low_hi, low_lo = split2(low)
    grad_hi, grad_lo = split2(low_grad)
    base = lax.psum_scatter(dot32(x, w, ((1,), (0,))), "tensor", scatter_dimension=1, tiled=True)
    adapter = dot32(low_hi, b, ((1,), (0,))) + dot32(low_lo, b, ((1,), (0,)))
    out_home = (base + SCALE * adapter).astype(jnp.bfloat16)
    sent = (
        jnp.zeros((groups * cap, length, columns), jnp.bfloat16)
        .at[index]
        .set(out_home.reshape(blocks, length, columns))
    )
    output = lax.all_to_all(
        sent.reshape(groups, cap * length, columns), "dp", split_axis=0, concat_axis=0, tiled=True
    ).reshape(dy.shape)
    full = lax.all_gather(dy_home, "tensor", axis=1, tiled=True)
    grad_home = (
        dot32(full, w, ((1,), (1,)))
        + dot32(grad_hi, a, ((1,), (1,)))
        + dot32(grad_lo, a, ((1,), (1,)))
    ).astype(jnp.bfloat16)
    a_term = dot32(x, grad_hi, ((0,), (0,))) + dot32(x, grad_lo, ((0,), (0,)))
    b_term = SCALE * (dot32(low_hi, dy_home, ((0,), (0,))) + dot32(low_lo, dy_home, ((0,), (0,))))
    return (
        output,
        grad_home,
        lax.psum_scatter(a_term, "dp", scatter_dimension=1, tiled=True),
        lax.psum_scatter(b_term, "dp", scatter_dimension=0, tiled=True),
    )


def local(*args):
    return general(*args)


def solution(mesh):
    return jax.shard_map(
        local,
        mesh=mesh,
        in_specs=(
            P(("parts", "dp"), "tensor"),
            P(("parts", "dp")),
            P(("parts", "dp")),
            P(("parts", "dp")),
            P("tensor", None),
            P("tensor", None),
            P(None, "tensor"),
            P(("parts", "dp"), "tensor"),
        ),
        out_specs=(
            P(("parts", "dp"), "tensor"),
            P(("parts", "dp"), "tensor"),
            P("tensor", ("parts", "dp")),
            P(("parts", "dp"), "tensor"),
        ),
        check_vma=False,
    )
```

```python
import functools

import jax
import jax.numpy as jnp
from jax import lax
from jax.experimental import pallas as pl
from jax.experimental.pallas import tpu as pltpu
from jax.sharding import PartitionSpec as P

ADAPTER_RANK = 16
SCALE = 2.0


def split2(v):
    high = lax.reduce_precision(v, 8, 7)
    return high.astype(jnp.bfloat16), (v - high).astype(jnp.bfloat16)


def dot32(a, b, dims):
    return lax.dot_general(a, b, (dims, ((), ())), preferred_element_type=jnp.float32)


def general(x, group, slot, job, w, a, b, dy):
    groups = lax.axis_size("dp")
    blocks = group.shape[0]
    rows, features = x.shape
    length = rows // blocks
    columns = dy.shape[1]
    cap = dy.shape[0] // length // groups
    jobs = a.shape[1] // ADAPTER_RANK
    index = group * cap + slot
    got = lax.all_to_all(
        dy.reshape(groups, cap * length, columns), "dp", split_axis=0, concat_axis=0, tiled=True
    )
    dy_home = got.reshape(groups * cap, length, columns)[index].reshape(rows, columns)
    hot = jnp.repeat(job, length)[:, None] == (
        jnp.arange(jobs * ADAPTER_RANK, dtype=jnp.int32) // ADAPTER_RANK
    )

    def of_job(terms):
        kept = jnp.where(hot, terms, 0.0).reshape(rows, jobs, ADAPTER_RANK)
        return jnp.sum(kept, axis=1).T

    def spread(sums):
        return jnp.where(hot, jnp.tile(sums.T, (1, jobs)), 0.0)

    parts = jnp.stack(
        (of_job(dot32(x, a, ((1,), (0,)))), of_job(SCALE * dot32(dy_home, b, ((1,), (1,)))))
    )
    sums = lax.psum(parts, "tensor")
    low, low_grad = spread(sums[0]), spread(sums[1])
    low_hi, low_lo = split2(low)
    grad_hi, grad_lo = split2(low_grad)
    base = lax.psum_scatter(dot32(x, w, ((1,), (0,))), "tensor", scatter_dimension=1, tiled=True)
    adapter = dot32(low_hi, b, ((1,), (0,))) + dot32(low_lo, b, ((1,), (0,)))
    out_home = (base + SCALE * adapter).astype(jnp.bfloat16)
    sent = (
        jnp.zeros((groups * cap, length, columns), jnp.bfloat16)
        .at[index]
        .set(out_home.reshape(blocks, length, columns))
    )
    output = lax.all_to_all(
        sent.reshape(groups, cap * length, columns), "dp", split_axis=0, concat_axis=0, tiled=True
    ).reshape(dy.shape)
    full = lax.all_gather(dy_home, "tensor", axis=1, tiled=True)
    grad_home = (
        dot32(full, w, ((1,), (1,)))
        + dot32(grad_hi, a, ((1,), (1,)))
        + dot32(grad_lo, a, ((1,), (1,)))
    ).astype(jnp.bfloat16)
    a_term = dot32(x, grad_hi, ((0,), (0,))) + dot32(x, grad_lo, ((0,), (0,)))
    b_term = SCALE * (dot32(low_hi, dy_home, ((0,), (0,))) + dot32(low_lo, dy_home, ((0,), (0,))))
    return (
        output,
        grad_home,
        lax.psum_scatter(a_term, "dp", scatter_dimension=1, tiled=True),
        lax.psum_scatter(b_term, "dp", scatter_dimension=0, tiled=True),
    )

RANGE = 32766.0
STEPS = 64.0
PAD = 16
VMEM_BYTES = 56 * 1024 * 1024


def params():
    return pltpu.CompilerParams(vmem_limit_bytes=VMEM_BYTES)


def cost(flops, read):
    return pl.CostEstimate(flops=flops, bytes_accessed=read, transcendentals=0)


def halves(v):
    high = v.astype(jnp.bfloat16)
    return high, (v - high.astype(jnp.float32)).astype(jnp.bfloat16)


def store_coded(out_ref, v):
    rows = v.shape[0]
    top = jnp.maximum(jnp.max(jnp.abs(v), axis=0, keepdims=True), 1e-30)
    level = jnp.ceil(jnp.log2(top) * STEPS)
    coded = jnp.round(v * (jnp.exp2(level * (-1.0 / STEPS)) * (RANGE * 0.9999)))
    out_ref[0, pl.ds(0, rows), :] = coded.astype(jnp.int32).astype(jnp.int16)
    out_ref[0, pl.ds(rows, PAD), :] = (
        jnp.broadcast_to(level, (PAD, v.shape[1])).astype(jnp.int32).astype(jnp.int16)
    )


def load_coded(in_ref):
    rows = in_ref.shape[1] - PAD
    level = in_ref[0, pl.ds(rows, PAD), :].astype(jnp.int32).astype(jnp.float32)[0:1, :]
    coded = in_ref[0, pl.ds(0, rows), :].astype(jnp.int32).astype(jnp.float32)
    return coded * (jnp.exp2(level * (1.0 / STEPS)) * (1.0 / (RANGE * 0.9999)))


def coded_spec(group_rows, columns):
    return pl.BlockSpec((1, group_rows + PAD, columns), lambda g, *_: (g, 0, 0))


def coded_shape(rows, group_rows, columns):
    return jax.ShapeDtypeStruct((rows // group_rows, group_rows + PAD, columns), jnp.int16)


def project(x, w, place, offsets, group_rows, columns, coded):
    rows, features = x.shape
    count = len(offsets)

    def kernel(place_ref, x_ref, *refs):
        weights = jnp.concatenate([r[...] for r in refs[:count]], axis=1)
        product = dot32(x_ref[...], weights, ((1,), (0,)))
        for i in range(count):
            part = product[:, i * columns : (i + 1) * columns]
            if coded:
                store_coded(refs[count + i], part)
            else:
                refs[count + i][...] = part

    def weight_spec(d):
        return pl.BlockSpec((features, columns), lambda g, place_ref: (0, place_ref[d]))

    if coded:
        out_specs = [coded_spec(group_rows, columns)] * count
        out_shape = [coded_shape(rows, group_rows, columns)] * count
    else:
        out_specs = [pl.BlockSpec((group_rows, columns), lambda g, place_ref: (g, 0))] * count
        out_shape = [jax.ShapeDtypeStruct((rows, columns), jnp.float32)] * count
    return pl.pallas_call(
        kernel,
        grid_spec=pltpu.PrefetchScalarGridSpec(
            num_scalar_prefetch=1,
            grid=(rows // group_rows,),
            in_specs=[pl.BlockSpec((group_rows, features), lambda g, place_ref: (g, 0))]
            + [weight_spec(d) for d in offsets],
            out_specs=out_specs,
        ),
        out_shape=out_shape,
        compiler_params=params(),
        cost_estimate=cost(
            2 * rows * features * columns * count, rows * features * 2 + rows * columns * 4 * count
        ),
        name="project",
    )(place, x, *([w] * count))


def add_coded(own, received, group_rows):
    rows, columns = own.shape

    def kernel(own_ref, received_ref, out_ref):
        store_coded(out_ref, own_ref[...] + load_coded(received_ref))

    return pl.pallas_call(
        kernel,
        grid=(rows // group_rows,),
        in_specs=[
            pl.BlockSpec((group_rows, columns), lambda g: (g, 0)),
            coded_spec(group_rows, columns),
        ],
        out_specs=coded_spec(group_rows, columns),
        out_shape=coded_shape(rows, group_rows, columns),
        compiler_params=params(),
        cost_estimate=cost(rows * columns, rows * columns * 8),
        name="add_coded",
    )(own, received)


SMEM = pl.BlockSpec(memory_space=pltpu.SMEM)
VMEM = pl.BlockSpec(memory_space=pltpu.VMEM)


def home_gradient(kept, received, b, group, slot, job, me, length):
    blocks = group.shape[0]
    columns = b.shape[1]

    def kernel(group_ref, slot_ref, job_ref, me_ref, kept_ref, received_ref, b_ref, dy_ref, low_ref):
        mine = me_ref[0]
        for n in range(blocks):
            at = pl.ds(pl.multiple_of(slot_ref[n] * length, length), length)

            @pl.when(group_ref[n] == mine)
            def _():
                dy_ref[pl.ds(n * length, length), :] = kept_ref[at, :]

            @pl.when(group_ref[n] != mine)
            def _():
                dy_ref[pl.ds(n * length, length), :] = received_ref[at, :]

            factor = b_ref[
                pl.ds(pl.multiple_of(job_ref[n] * ADAPTER_RANK, ADAPTER_RANK), ADAPTER_RANK), :
            ]
            low_ref[n] = SCALE * dot32(
                factor, dy_ref[pl.ds(n * length, length), :], ((1,), (1,))
            )

    return pl.pallas_call(
        kernel,
        in_specs=[SMEM] * 4 + [VMEM] * 3,
        out_specs=[VMEM, VMEM],
        out_shape=[
            jax.ShapeDtypeStruct((blocks * length, columns), jnp.bfloat16),
            jax.ShapeDtypeStruct((blocks, ADAPTER_RANK, length), jnp.float32),
        ],
        compiler_params=params(),
        cost_estimate=cost(2 * blocks * length * columns * ADAPTER_RANK, 4 * kept.size * 2),
        name="home_gradient",
    )(group, slot, job, me, kept, received, b)


def low_rank(x, a_t, job, length, step_blocks):
    blocks = job.shape[0]
    features = x.shape[1]

    def kernel(job_ref, x_ref, a_ref, low_ref):
        first = pl.program_id(0) * step_blocks
        for i in range(step_blocks):
            factor = a_ref[
                pl.ds(
                    pl.multiple_of(job_ref[first + i] * ADAPTER_RANK, ADAPTER_RANK), ADAPTER_RANK
                ),
                :,
            ]
            low_ref[i] = dot32(factor, x_ref[pl.ds(i * length, length), :], ((1,), (1,)))

    return pl.pallas_call(
        kernel,
        grid_spec=pltpu.PrefetchScalarGridSpec(
            num_scalar_prefetch=1,
            grid=(blocks // step_blocks,),
            in_specs=[
                pl.BlockSpec((step_blocks * length, features), lambda g, job_ref: (g, 0)),
                pl.BlockSpec(a_t.shape, lambda g, job_ref: (0, 0)),
            ],
            out_specs=pl.BlockSpec(
                (step_blocks, ADAPTER_RANK, length), lambda g, job_ref: (g, 0, 0)
            ),
        ),
        out_shape=jax.ShapeDtypeStruct((blocks, ADAPTER_RANK, length), jnp.float32),
        compiler_params=params(),
        cost_estimate=cost(2 * x.size * ADAPTER_RANK, x.size * 2),
        name="low_rank",
    )(job, x, a_t)


def factor_gradients(x, dy_home, low, low_grad, job, jobs, length, step_blocks):
    blocks = job.shape[0]
    features = x.shape[1]
    columns = dy_home.shape[1]

    def kernel(job_ref, x_ref, dy_ref, low_ref, grad_ref, out_ref):
        step = pl.program_id(0)

        @pl.when(step == 0)
        def _():
            out_ref[...] = jnp.zeros_like(out_ref)

        for i in range(step_blocks):
            at = pl.ds(
                pl.multiple_of(job_ref[step * step_blocks + i] * ADAPTER_RANK, ADAPTER_RANK),
                ADAPTER_RANK,
            )
            here = pl.ds(i * length, length)
            terms = dot32(
                jnp.concatenate(halves(grad_ref[i]), axis=0), x_ref[here, :], ((1,), (0,))
            )
            out_ref[at, pl.ds(0, features)] += terms[:ADAPTER_RANK] + terms[ADAPTER_RANK:]
            terms = dot32(
                jnp.concatenate(halves(SCALE * low_ref[i]), axis=0), dy_ref[here, :], ((1,), (0,))
            )
            out_ref[at, pl.ds(features, columns)] += terms[:ADAPTER_RANK] + terms[ADAPTER_RANK:]

    low_spec = pl.BlockSpec((step_blocks, ADAPTER_RANK, length), lambda g, job_ref: (g, 0, 0))
    shape = (jobs * ADAPTER_RANK, features + columns)
    return pl.pallas_call(
        kernel,
        grid_spec=pltpu.PrefetchScalarGridSpec(
            num_scalar_prefetch=1,
            grid=(blocks // step_blocks,),
            in_specs=[
                pl.BlockSpec((step_blocks * length, features), lambda g, job_ref: (g, 0)),
                pl.BlockSpec((step_blocks * length, columns), lambda g, job_ref: (g, 0)),
                low_spec,
                low_spec,
            ],
            out_specs=pl.BlockSpec(shape, lambda g, job_ref: (0, 0)),
        ),
        out_shape=jax.ShapeDtypeStruct(shape, jnp.float32),
        compiler_params=params(),
        cost_estimate=cost(8 * x.size * ADAPTER_RANK, x.size * 2),
        name="factor_gradients",
    )(job, x, dy_home, low, low_grad)


def place_output(own, from_left, from_right, low, b, group, slot, job, me, length, cap):
    blocks = group.shape[0]
    columns = b.shape[1]
    group_rows = from_left.shape[1] - PAD
    per_group = group_rows // length

    def kernel(
        group_ref, slot_ref, job_ref, me_ref, own_ref, left_ref, right_ref, low_ref, b_ref, out_ref
    ):
        out_ref[...] = jnp.zeros_like(out_ref)
        for g in range(blocks // per_group):
            scales = []
            for ref in (left_ref, right_ref):
                level = ref[g, pl.ds(group_rows, PAD), :].astype(jnp.int32).astype(jnp.float32)
                scales.append(
                    jnp.exp2(level[0:1, :] * (1.0 / STEPS)) * (1.0 / (RANGE * 0.9999))
                )
            for i in range(per_group):
                n = g * per_group + i
                total = own_ref[pl.ds(n * length, length), :]
                for ref, scale in zip((left_ref, right_ref), scales):
                    coded = ref[g, pl.ds(i * length, length), :].astype(jnp.int32)
                    total = total + coded.astype(jnp.float32) * scale
                factor = b_ref[
                    pl.ds(pl.multiple_of(job_ref[n] * ADAPTER_RANK, ADAPTER_RANK), ADAPTER_RANK), :
                ]
                high, rest = halves((SCALE * low_ref[n]).T)
                total = total + (
                    dot32(high, factor, ((1,), (0,))) + dot32(rest, factor, ((1,), (0,)))
                )
                other = jnp.where(group_ref[n] == me_ref[0], 0, 1)
                out_ref[other * cap + slot_ref[n]] = total.astype(jnp.bfloat16)

    return pl.pallas_call(
        kernel,
        in_specs=[SMEM] * 4 + [VMEM] * 5,
        out_specs=VMEM,
        out_shape=jax.ShapeDtypeStruct((2 * cap, length, columns), jnp.bfloat16),
        compiler_params=params(),
        cost_estimate=cost(own.size * 64, own.size * 10),
        name="place_output",
    )(group, slot, job, me, own, from_left, from_right, low, b)


def input_gradient(pieces, w_rows, low_grad, a_t, job, length, step_blocks):
    blocks = job.shape[0]
    columns = pieces[0].shape[1]
    features = a_t.shape[1]
    count = len(pieces)

    def kernel(job_ref, *refs):
        w_ref, grad_ref, a_ref, out_ref = refs[count:]
        lhs = jnp.concatenate([r[...] for r in refs[:count]], axis=1)
        total = dot32(lhs, w_ref[...], ((1,), (0,)))
        for i in range(step_blocks):
            n = pl.program_id(0) * step_blocks + i
            factor = a_ref[
                pl.ds(pl.multiple_of(job_ref[n] * ADAPTER_RANK, ADAPTER_RANK), ADAPTER_RANK), :
            ]
            high, rest = halves(grad_ref[i].T)
            here = slice(i * length, (i + 1) * length)
            out_ref[pl.ds(i * length, length), :] = (
                total[here]
                + (dot32(high, factor, ((1,), (0,))) + dot32(rest, factor, ((1,), (0,))))
            ).astype(jnp.bfloat16)

    rows = blocks * length
    step_rows = step_blocks * length
    return pl.pallas_call(
        kernel,
        grid_spec=pltpu.PrefetchScalarGridSpec(
            num_scalar_prefetch=1,
            grid=(blocks // step_blocks,),
            in_specs=[pl.BlockSpec((step_rows, columns), lambda g, job_ref: (g, 0))] * count
            + [
                pl.BlockSpec(w_rows.shape, lambda g, job_ref: (0, 0)),
                pl.BlockSpec(
                    (step_blocks, ADAPTER_RANK, length), lambda g, job_ref: (g, 0, 0)
                ),
                pl.BlockSpec(a_t.shape, lambda g, job_ref: (0, 0)),
            ],
            out_specs=pl.BlockSpec((step_rows, features), lambda g, job_ref: (g, 0)),
        ),
        out_shape=jax.ShapeDtypeStruct((rows, features), jnp.bfloat16),
        compiler_params=params(),
        cost_estimate=cost(2 * rows * features * columns * count, rows * features * 4),
        name="input_gradient",
    )(job, *pieces, w_rows, low_grad, a_t)


def ring(x, group, slot, job, w, a, b, dy):
    size = lax.axis_size("tensor")
    me = lax.axis_index("dp").astype(jnp.int32)
    blocks = group.shape[0]
    rows, features = x.shape
    length = rows // blocks
    columns = dy.shape[1]
    half = dy.shape[0] // 2
    cap = half // length
    jobs = a.shape[1] // ADAPTER_RANK
    step_blocks = 8
    group_rows = step_blocks * length

    order = [2 * r for r in range(size // 2)] + [2 * r + 1 for r in reversed(range(size // 2))]
    place_of = [order.index(t) for t in range(size)]
    here = jnp.asarray(place_of, jnp.int32)[lax.axis_index("tensor")]
    place = jnp.asarray(order, jnp.int32)[(here + jnp.arange(size, dtype=jnp.int32)) % size]
    ahead = [(order[r], order[(r + 1) % size]) for r in range(size)]
    back = [(order[r], order[(r - 1) % size]) for r in range(size)]
    swap = [(0, 1), (1, 0)]

    def right(v):
        return lax.ppermute(v, "tensor", ahead)

    def left(v):
        return lax.ppermute(v, "tensor", back)

    mine = me[None]
    kept = lax.dynamic_slice_in_dim(dy, me * half, half)
    got = lax.ppermute(lax.dynamic_slice_in_dim(dy, (1 - me) * half, half), "dp", swap)

    far, near = size // 2, size // 2 - 1
    sums_r, sums_l = project(x, w, place, (far, size - near), group_rows, columns, True)
    sums_r = right(sums_r)
    sums_l = left(sums_l)
    dy_home, low_grad = home_gradient(kept, got, b, group, slot, job, mine, length)
    held_r = right(dy_home)
    held_l = left(dy_home)
    a_t = a.T
    low = low_rank(x, a_t, job, length, step_blocks)
    low, low_grad = lax.psum((low, low_grad), "tensor")

    offsets = []
    for d in range(1, far):
        offsets += [far - d] + ([size - (near - d)] if near > d else [])
    offsets += [0]
    terms = dict(zip(offsets, project(x, w, place, tuple(offsets), group_rows, columns, False)))

    pieces = {0: dy_home, size - 1: held_r, 1: held_l}
    for d in range(1, far):
        sums_r = right(add_coded(terms[far - d], sums_r, group_rows))
        if near > d:
            sums_l = left(add_coded(terms[size - (near - d)], sums_l, group_rows))
        if d < near:
            held_r = right(held_r)
            pieces[size - 1 - d] = held_r
        held_l = left(held_l)
        pieces[1 + d] = held_l

    factors = factor_gradients(x, dy_home, low, low_grad, job, jobs, length, step_blocks)
    part = factors.shape[0] // 2
    theirs = lax.ppermute(lax.dynamic_slice_in_dim(factors, (1 - me) * part, part), "dp", swap)
    factors = lax.dynamic_slice_in_dim(factors, me * part, part) + theirs

    placed = place_output(
        terms[0], sums_r, sums_l, low, b, group, slot, job, mine, length, cap
    ).reshape(2, half, columns)
    theirs = lax.ppermute(placed[1], "dp", swap)
    output = jnp.where(
        me == 0,
        jnp.concatenate((placed[0], theirs)),
        jnp.concatenate((theirs, placed[0])),
    )

    w_rows = w.T.reshape(size, columns, features)[place].reshape(size * columns, features)
    grad_home = input_gradient(
        [pieces[d] for d in range(size)], w_rows, low_grad, a_t, job, length, step_blocks // 2
    )
    return output, grad_home, factors[:, :features].T, factors[:, features:]


def local(*args):
    x, group, dy = args[0], args[1], args[7]
    size = lax.axis_size("tensor")
    blocks = group.shape[0]
    length = x.shape[0] // blocks
    fits = (
        lax.axis_size("dp") == 2
        and size % 2 == 0
        and 4 <= size <= 8
        and dy.shape[1] % 128 == 0
        and x.shape[1] % 128 == 0
        and length % 128 == 0
        and blocks % 8 == 0
    )
    return ring(*args) if fits else general(*args)


def solution(mesh):
    return jax.shard_map(
        local,
        mesh=mesh,
        in_specs=(
            P(("parts", "dp"), "tensor"),
            P(("parts", "dp")),
            P(("parts", "dp")),
            P(("parts", "dp")),
            P("tensor", None),
            P("tensor", None),
            P(None, "tensor"),
            P(("parts", "dp"), "tensor"),
        ),
        out_specs=(
            P(("parts", "dp"), "tensor"),
            P(("parts", "dp"), "tensor"),
            P("tensor", ("parts", "dp")),
            P(("parts", "dp"), "tensor"),
        ),
        check_vma=False,
    )
```

```python
import functools

import jax
import jax.numpy as jnp
from jax import lax
from jax.experimental import pallas as pl
from jax.experimental.pallas import tpu as pltpu
from jax.sharding import PartitionSpec as P

ADAPTER_RANK = 16
SCALE = 2.0


def split2(v):
    high = lax.reduce_precision(v, 8, 7)
    return high.astype(jnp.bfloat16), (v - high).astype(jnp.bfloat16)


def dot32(a, b, dims):
    return lax.dot_general(a, b, (dims, ((), ())), preferred_element_type=jnp.float32)


def general(x, group, slot, job, w, a, b, dy):
    groups = lax.axis_size("dp")
    blocks = group.shape[0]
    rows, features = x.shape
    length = rows // blocks
    columns = dy.shape[1]
    cap = dy.shape[0] // length // groups
    jobs = a.shape[1] // ADAPTER_RANK
    index = group * cap + slot
    got = lax.all_to_all(
        dy.reshape(groups, cap * length, columns), "dp", split_axis=0, concat_axis=0, tiled=True
    )
    dy_home = got.reshape(groups * cap, length, columns)[index].reshape(rows, columns)
    hot = jnp.repeat(job, length)[:, None] == (
        jnp.arange(jobs * ADAPTER_RANK, dtype=jnp.int32) // ADAPTER_RANK
    )

    def of_job(terms):
        kept = jnp.where(hot, terms, 0.0).reshape(rows, jobs, ADAPTER_RANK)
        return jnp.sum(kept, axis=1).T

    def spread(sums):
        return jnp.where(hot, jnp.tile(sums.T, (1, jobs)), 0.0)

    parts = jnp.stack(
        (of_job(dot32(x, a, ((1,), (0,)))), of_job(SCALE * dot32(dy_home, b, ((1,), (1,)))))
    )
    sums = lax.psum(parts, "tensor")
    low, low_grad = spread(sums[0]), spread(sums[1])
    low_hi, low_lo = split2(low)
    grad_hi, grad_lo = split2(low_grad)
    base = lax.psum_scatter(dot32(x, w, ((1,), (0,))), "tensor", scatter_dimension=1, tiled=True)
    adapter = dot32(low_hi, b, ((1,), (0,))) + dot32(low_lo, b, ((1,), (0,)))
    out_home = (base + SCALE * adapter).astype(jnp.bfloat16)
    sent = (
        jnp.zeros((groups * cap, length, columns), jnp.bfloat16)
        .at[index]
        .set(out_home.reshape(blocks, length, columns))
    )
    output = lax.all_to_all(
        sent.reshape(groups, cap * length, columns), "dp", split_axis=0, concat_axis=0, tiled=True
    ).reshape(dy.shape)
    full = lax.all_gather(dy_home, "tensor", axis=1, tiled=True)
    grad_home = (
        dot32(full, w, ((1,), (1,)))
        + dot32(grad_hi, a, ((1,), (1,)))
        + dot32(grad_lo, a, ((1,), (1,)))
    ).astype(jnp.bfloat16)
    a_term = dot32(x, grad_hi, ((0,), (0,))) + dot32(x, grad_lo, ((0,), (0,)))
    b_term = SCALE * (dot32(low_hi, dy_home, ((0,), (0,))) + dot32(low_lo, dy_home, ((0,), (0,))))
    return (
        output,
        grad_home,
        lax.psum_scatter(a_term, "dp", scatter_dimension=1, tiled=True),
        lax.psum_scatter(b_term, "dp", scatter_dimension=0, tiled=True),
    )

RANGE = 32766.0
STEPS = 64.0
PAD = 16
VMEM_BYTES = 63 * 1024 * 1024


SMEM = pl.BlockSpec(memory_space=pltpu.SMEM)
VMEM = pl.BlockSpec(memory_space=pltpu.VMEM)
ANY = pl.BlockSpec(memory_space=pl.ANY)


def params():
    return pltpu.CompilerParams(vmem_limit_bytes=VMEM_BYTES)


def cost():
    return pl.CostEstimate(flops=1, bytes_accessed=1, transcendentals=0)


def halves(v):
    high = v.astype(jnp.bfloat16)
    return high, (v - high.astype(jnp.float32)).astype(jnp.bfloat16)


def store_coded(out_ref, at, v):
    rows = v.shape[0]
    top = jnp.maximum(jnp.max(jnp.abs(v), axis=0, keepdims=True), 1e-30)
    level = jnp.ceil(jnp.log2(top) * STEPS)
    coded = jnp.round(v * (jnp.exp2(level * (-1.0 / STEPS)) * (RANGE * 0.9999)))
    out_ref[at, pl.ds(0, rows), :] = coded.astype(jnp.int32).astype(jnp.int16)
    out_ref[at, pl.ds(rows, PAD), :] = (
        jnp.broadcast_to(level, (PAD, v.shape[1])).astype(jnp.int32).astype(jnp.int16)
    )


def load_coded(in_ref, at, first=0, rows=None):
    total = in_ref.shape[1] - PAD
    level = in_ref[at, pl.ds(total, PAD), :].astype(jnp.int32).astype(jnp.float32)[0:1, :]
    coded = in_ref[at, pl.ds(first, rows or total), :].astype(jnp.int32).astype(jnp.float32)
    return coded * (jnp.exp2(level * (1.0 / STEPS)) * (1.0 / (RANGE * 0.9999)))


LANES = 128
PACKED = LANES // ADAPTER_RANK


def lane_slot(shape):
    return lax.broadcasted_iota(jnp.int32, shape, len(shape) - 1) // ADAPTER_RANK


def pack(tile, i, values, job):
    kept = values[:, :LANES]
    for h in range(1, values.shape[1] // LANES):
        kept = jnp.where(job // PACKED == h, values[:, h * LANES : (h + 1) * LANES], kept)
    shift = lax.rem((i - lax.rem(job, PACKED) + PACKED) * ADAPTER_RANK, LANES)
    return jnp.where(lane_slot(tile.shape) == i, pltpu.roll(kept, shift, 1), tile)


def expand(tile, i, job, columns):
    place = lax.rem(job, PACKED)
    shift = lax.rem((place - i + PACKED) * ADAPTER_RANK, LANES)
    rolled = pltpu.roll(tile, shift, 1)
    rolled = jnp.where(lane_slot(tile.shape) == place, rolled, 0.0)
    return jnp.concatenate(
        [jnp.where(job // PACKED == h, rolled, 0.0) for h in range(columns // LANES)], axis=1
    )


def coded_spec(group_rows, columns):
    return pl.BlockSpec((1, group_rows + PAD, columns), lambda g, *_: (g, 0, 0))


def coded_shape(rows, group_rows, columns):
    return jax.ShapeDtypeStruct((rows // group_rows, group_rows + PAD, columns), jnp.int16)


def project(x, first, rows, w, place, offsets, group_rows, columns, coded, after=()):
    features = x.shape[1]
    count = len(offsets)
    start = first // group_rows

    def kernel(place_ref, x_ref, *refs):
        weight_ref = refs[-1]
        refs = refs[:count] + refs[count + len(after) : -1]

        @pl.when(pl.program_id(0) == 0)
        def _():
            for i in range(count):
                weight_ref[:, i * columns : (i + 1) * columns] = refs[i][...]

        product = dot32(x_ref[...], weight_ref[...], ((1,), (0,)))
        for i in range(count):
            part = product[:, i * columns : (i + 1) * columns]
            if coded:
                store_coded(refs[count + i], 0, part)
            else:
                refs[count + i][...] = part

    def weight_spec(d):
        return pl.BlockSpec((features, columns), lambda g, place_ref: (0, place_ref[d]))

    if coded:
        out_specs = [coded_spec(group_rows, columns)] * count
        out_shape = [coded_shape(rows, group_rows, columns)] * count
    else:
        out_specs = [pl.BlockSpec((group_rows, columns), lambda g, place_ref: (g, 0))] * count
        out_shape = [jax.ShapeDtypeStruct((rows, columns), jnp.float32)] * count
    return pl.pallas_call(
        kernel,
        grid_spec=pltpu.PrefetchScalarGridSpec(
            num_scalar_prefetch=1,
            grid=(rows // group_rows,),
            in_specs=[pl.BlockSpec((group_rows, features), lambda g, place_ref: (g + start, 0))]
            + [weight_spec(d) for d in offsets]
            + [ANY] * len(after),
            out_specs=out_specs,
            scratch_shapes=[pltpu.VMEM((features, count * columns), jnp.bfloat16)],
        ),
        out_shape=out_shape,
        compiler_params=params(),
        cost_estimate=cost(),
        name="project",
    )(place, x, *([w] * count), *after)


def add_coded(pairs, group_rows, after, sums=False, coded=True, groups=1):
    rows, columns = pairs[0][0].shape
    count = len(pairs)

    def kernel(*refs):
        outs = refs[2 * count + len(after) :]
        for p in range(count):
            for g in range(groups):
                here = pl.ds(g * group_rows, group_rows)
                total = refs[2 * p][here, :] + load_coded(refs[2 * p + 1], g)
                if sums:
                    outs[p][here, :] = total
                if coded:
                    store_coded(outs[count * sums + p], g, total)

    block = pl.BlockSpec((groups * group_rows, columns), lambda g: (g, 0))
    coded_block = pl.BlockSpec((groups, group_rows + PAD, columns), lambda g: (g, 0, 0))
    return pl.pallas_call(
        kernel,
        grid=(rows // group_rows // groups,),
        in_specs=[block, coded_block] * count + [ANY] * len(after),
        out_specs=[block] * (count * sums) + [coded_block] * (count * coded),
        out_shape=[jax.ShapeDtypeStruct((rows, columns), jnp.float32)] * (count * sums)
        + [coded_shape(rows, group_rows, columns)] * (count * coded),
        compiler_params=params(),
        cost_estimate=cost(),
        name="add_coded",
    )(*[v for pair in pairs for v in pair], *after)


def home_gradient(dy, received, group, slot, me, length, streams, after):
    blocks = group.shape[0]
    columns = dy.shape[1]
    half = received.shape[0]
    per = blocks // streams

    def kernel(group_ref, slot_ref, me_ref, dy_ref, received_ref, *refs):
        outs = refs[len(after) :]
        mine = me_ref[0]

        def put(n, value):
            outs[0][pl.ds(n * length, length), :] = value
            outs[1 + n // per][pl.ds(n % per * length, length), :] = value

        for n in range(blocks):
            at = slot_ref[n] * length

            @pl.when(group_ref[n] == mine)
            def _():
                put(n, dy_ref[pl.ds(pl.multiple_of(mine * half + at, length), length), :])

            @pl.when(group_ref[n] != mine)
            def _():
                put(n, received_ref[pl.ds(pl.multiple_of(at, length), length), :])

    return pl.pallas_call(
        kernel,
        in_specs=[SMEM] * 3 + [VMEM] * 2 + [ANY] * len(after),
        out_specs=[VMEM] * (1 + streams),
        out_shape=[jax.ShapeDtypeStruct((blocks * length, columns), jnp.bfloat16)]
        + [jax.ShapeDtypeStruct((per * length, columns), jnp.bfloat16)] * streams,
        compiler_params=params(),
        cost_estimate=cost(),
        name="home_gradient",
    )(group, slot, me, dy, received, *after)


def low_rank(x, a, dy_home, b_t, job, length, after):
    blocks = job.shape[0]
    features = x.shape[1]
    columns = dy_home.shape[1]

    def kernel(job_ref, x_ref, a_ref, dy_ref, b_ref, *refs):
        low_ref, coded_ref = refs[-2:]
        first = pl.program_id(0) * PACKED
        products = (
            dot32(x_ref[...], a_ref[...], ((1,), (0,))),
            SCALE * dot32(dy_ref[...], b_ref[...], ((1,), (0,))),
        )
        for kind, product in enumerate(products):
            tile = jnp.zeros((length, LANES), jnp.float32)
            for i in range(PACKED):
                tile = pack(tile, i, product[i * length : (i + 1) * length], job_ref[first + i])
            low_ref[pl.ds(kind * length, length), :] = tile
            store_coded(coded_ref, kind, tile)

    rows = PACKED * length
    return pl.pallas_call(
        kernel,
        grid_spec=pltpu.PrefetchScalarGridSpec(
            num_scalar_prefetch=1,
            grid=(blocks // PACKED,),
            in_specs=[
                pl.BlockSpec((rows, features), lambda g, job_ref: (g, 0)),
                pl.BlockSpec(a.shape, lambda g, job_ref: (0, 0)),
                pl.BlockSpec((rows, columns), lambda g, job_ref: (g, 0)),
                pl.BlockSpec(b_t.shape, lambda g, job_ref: (0, 0)),
            ]
            + [ANY] * len(after),
            out_specs=[
                pl.BlockSpec((2 * length, LANES), lambda g, job_ref: (g, 0)),
                pl.BlockSpec((2, length + PAD, LANES), lambda g, job_ref: (g, 0, 0)),
            ],
        ),
        out_shape=[
            jax.ShapeDtypeStruct((blocks // PACKED * 2 * length, LANES), jnp.float32),
            coded_shape(blocks // PACKED * 2 * length, length, LANES),
        ],
        compiler_params=params(),
        cost_estimate=cost(),
        name="low_rank",
    )(job, x, a, dy_home, b_t, *after)


def factor_gradients(x, dy_home, low, job, ranks, length, after):
    blocks = job.shape[0]
    features = x.shape[1]
    columns = dy_home.shape[1]

    def kernel(job_ref, x_ref, dy_ref, low_ref, *refs):
        out_ref = refs[-1]
        step = pl.program_id(0)
        spread = []
        for kind in range(2):
            tile = low_ref[pl.ds(kind * length, length), :]
            wide = jnp.concatenate(
                [expand(tile, i, job_ref[step * PACKED + i], ranks) for i in range(PACKED)], axis=0
            )
            spread.append(jnp.concatenate(halves(wide), axis=1))
        down = dot32(spread[1], x_ref[...], ((0,), (0,)))
        up = SCALE * dot32(spread[0], dy_ref[...], ((0,), (0,)))

        @pl.when(step == 0)
        def _():
            out_ref[...] = jnp.zeros_like(out_ref)

        out_ref[:, pl.ds(0, features)] += down[:ranks] + down[ranks:]
        out_ref[:, pl.ds(features, columns)] += up[:ranks] + up[ranks:]

    rows = PACKED * length
    shape = (ranks, features + columns)
    return pl.pallas_call(
        kernel,
        grid_spec=pltpu.PrefetchScalarGridSpec(
            num_scalar_prefetch=1,
            grid=(blocks // PACKED,),
            in_specs=[
                pl.BlockSpec((rows, features), lambda g, job_ref: (g, 0)),
                pl.BlockSpec((rows, columns), lambda g, job_ref: (g, 0)),
                pl.BlockSpec((2 * length, LANES), lambda g, job_ref: (g, 0)),
            ]
            + [ANY] * len(after),
            out_specs=pl.BlockSpec(shape, lambda g, job_ref: (0, 0)),
        ),
        out_shape=jax.ShapeDtypeStruct(shape, jnp.float32),
        compiler_params=params(),
        cost_estimate=cost(),
        name="factor_gradients",
    )(job, x, dy_home, low, *after)


def place_output(own, from_left, from_right, low, b, group, slot, job, me, length, cap, after):
    blocks = group.shape[0]
    ranks, columns = b.shape
    per_group = (from_left[0].shape[1] - PAD) // length
    count = len(own)
    per_stream = blocks // count

    def kernel(group_ref, slot_ref, job_ref, me_ref, low_ref, b_ref, *refs):
        out_ref = refs[-1]
        out_ref[...] = jnp.zeros_like(out_ref)
        factors = jnp.concatenate((b_ref[...], b_ref[...]), axis=0)
        for n in range(blocks):
            own_ref, left_ref, right_ref = refs[3 * (n // per_stream) :][:3]
            m = n % per_stream
            g, i = m // per_group, m % per_group
            total = (
                own_ref[pl.ds(m * length, length), :]
                + load_coded(left_ref, g, i * length, length)
                + load_coded(right_ref, g, i * length, length)
            )
            tile = low_ref[pl.ds(n // PACKED * 2 * length, length), :]
            wide = jnp.concatenate(
                halves(expand(SCALE * tile, n % PACKED, job_ref[n], ranks)), axis=1
            )
            total = total + dot32(wide, factors, ((1,), (0,)))
            other = jnp.where(group_ref[n] == me_ref[0], 0, 1)
            out_ref[other * cap + slot_ref[n]] = total.astype(jnp.bfloat16)

    sums = [v for k in range(count) for v in (own[k], from_left[k], from_right[k])]
    return pl.pallas_call(
        kernel,
        in_specs=[SMEM] * 4 + [VMEM] * (2 + len(sums)) + [ANY] * len(after),
        out_specs=VMEM,
        out_shape=jax.ShapeDtypeStruct((2 * cap, length, columns), jnp.bfloat16),
        compiler_params=params(),
        cost_estimate=cost(),
        name="place_output",
    )(group, slot, job, me, low, b, *sums, *after)


def input_gradient(pieces, w_t, place, low, a_t, job, length, step_blocks, stream, made, after):
    blocks = job.shape[0]
    count = len(pieces)
    stream_rows, columns = pieces[0].shape
    ranks, features = a_t.shape
    depth = count * columns + 2 * ranks
    steps = stream_rows // (step_blocks * length)
    start = stream * steps
    held = () if made is None else (made,)

    def kernel(job_ref, place_ref, *refs):
        weights, parts = refs[:count], refs[count : 2 * count]
        low_ref, a_ref = refs[2 * count : 2 * count + 2]
        out_ref, factor_ref = refs[-2:]

        @pl.when(pl.program_id(0) == 0)
        def _():
            for i in range(count):
                factor_ref[pl.ds(i * columns, columns), :] = weights[i][...]
            for i in range(2):
                factor_ref[pl.ds(count * columns + i * ranks, ranks), :] = a_ref[...]

        wide = []
        for i in range(step_blocks):
            n = (pl.program_id(0) + start) * step_blocks + i
            first = pl.multiple_of((2 * (n // PACKED) + 1) * length, length)
            tile = low_ref[pl.ds(first, length), :]
            wide.append(expand(tile, lax.rem(n, PACKED), job_ref[n], ranks))
        lhs = [r[...] for r in parts] + list(halves(jnp.concatenate(wide, axis=0)))
        out_ref[...] = dot32(
            jnp.concatenate(lhs, axis=1), factor_ref[...], ((1,), (0,))
        ).astype(jnp.bfloat16)

    step_rows = step_blocks * length

    def weight_spec(d):
        return pl.BlockSpec((columns, features), lambda g, job_ref, place_ref: (place_ref[d], 0))

    def whole_spec(v):
        return pl.BlockSpec(v.shape, lambda g, job_ref, place_ref: (0, 0))

    return pl.pallas_call(
        kernel,
        grid_spec=pltpu.PrefetchScalarGridSpec(
            num_scalar_prefetch=2,
            grid=(steps,),
            in_specs=[weight_spec(d) for d in range(count)]
            + [pl.BlockSpec((step_rows, columns), lambda g, job_ref, place_ref: (g, 0))] * count
            + [whole_spec(low), whole_spec(a_t)]
            + [ANY] * (len(held) + len(after)),
            out_specs=pl.BlockSpec(
                (step_rows, features), lambda g, job_ref, place_ref: (g + start, 0)
            ),
            scratch_shapes=[pltpu.VMEM((depth, features), jnp.bfloat16)],
        ),
        out_shape=jax.ShapeDtypeStruct((blocks * length, features), jnp.bfloat16),
        input_output_aliases={2 + 2 * count + 2: 0} if held else {},
        compiler_params=params(),
        cost_estimate=cost(),
        name="input_gradient",
    )(job, place, *([w_t] * count), *[pieces[d] for d in range(count)], low, a_t, *held, *after)


def ring(x, group, slot, job, w, a, b, dy):
    size = lax.axis_size("tensor")
    me = lax.axis_index("dp").astype(jnp.int32)
    blocks = group.shape[0]
    rows, features = x.shape
    length = rows // blocks
    columns = dy.shape[1]
    half = dy.shape[0] // 2
    cap = half // length
    streams = 2
    part_rows = rows // streams
    step_blocks = blocks // streams // 2
    group_rows = step_blocks * length

    order = [2 * r for r in range(size // 2)] + [2 * r + 1 for r in reversed(range(size // 2))]
    me_tensor = lax.axis_index("tensor").astype(jnp.int32)
    here = jnp.where(me_tensor % 2 == 0, me_tensor // 2, size - 1 - me_tensor // 2)
    there = (here + jnp.arange(size, dtype=jnp.int32)) % size
    place = jnp.where(there < size // 2, 2 * there, 2 * (size - 1 - there) + 1)
    ahead = [(order[r], order[(r + 1) % size]) for r in range(size)]
    back = [(order[r], order[(r - 1) % size]) for r in range(size)]
    swap = [(0, 1), (1, 0)]

    def right(v):
        return lax.ppermute(v, "tensor", ahead)

    def left(v):
        return lax.ppermute(v, "tensor", back)

    def exchange(v, bit):
        return lax.ppermute(v, "tensor", [(t, t ^ bit) for t in range(size)])

    mine = me[None]
    got = lax.ppermute(lax.dynamic_slice_in_dim(dy, (1 - me) * half, half), "dp", swap)

    far, near = size // 2, size // 2 - 1
    both = range(streams)
    sums_r, sums_l, held_r, held_l, terms, pieces = [], [], [], [], [], []
    last = ()

    def first(k):
        nonlocal last
        r, l = project(
            x, k * part_rows, part_rows, w, place, (far, size - near), group_rows, columns, True, last
        )
        last = (r,)
        sums_r.append(right(r))
        sums_l.append(left(l))

    first(0)
    dy_home, *parts = home_gradient(dy, got, group, slot, mine, length, streams, last)
    for k in both:
        held_r.append(right(parts[k]))
        held_l.append(left(parts[k]))
        pieces.append({0: parts[k], size - 1: held_r[k], 1: held_l[k]})
    last = (dy_home,)
    for k in both[1:]:
        first(k)
    low, coded = low_rank(x, a, dy_home, b.T, job, length, last)
    last = (coded,)
    bit = 1
    swapped = exchange(coded, bit)

    offsets = []
    for d in range(1, far):
        offsets += [far - d] + ([size - (near - d)] if near > d else [])
    offsets += [0]
    for k in both:
        made = project(
            x, k * part_rows, part_rows, w, place, tuple(offsets), group_rows, columns, False, last
        )
        terms.append(dict(zip(offsets, made)))
        last = (made[0],)

    def low_step():
        nonlocal low, swapped, bit, last
        more = 2 * bit < size
        got = add_coded([(low, swapped)], length, last, True, more, low.shape[0] // length)
        low = got[0]
        last = (low,)
        bit *= 2
        if more:
            swapped = exchange(got[1], bit)

    low_step()
    for d in range(1, far):
        for k in both:
            pairs = [(terms[k][far - d], sums_r[k])]
            if near > d:
                pairs.append((terms[k][size - (near - d)], sums_l[k]))
            turns = add_coded(pairs, group_rows, last)
            sums_r[k] = right(turns[0])
            if near > d:
                sums_l[k] = left(turns[1])
            last = (turns[0], held_l[k])
            if d < near:
                last += (held_r[k],)
                held_r[k] = right(held_r[k])
                pieces[k][size - 1 - d] = held_r[k]
            held_l[k] = left(held_l[k])
            pieces[k][1 + d] = held_l[k]
        if bit < size:
            low_step()

    ranks = a.shape[1]
    factors = factor_gradients(x, dy_home, low, job, ranks, length, last)
    part = ranks // 2
    theirs = lax.ppermute(lax.dynamic_slice_in_dim(factors, (1 - me) * part, part), "dp", swap)
    w_t, a_t = w.T, a.T
    placed = place_output(
        [terms[k][0] for k in both], sums_r, sums_l, low, b, group, slot, job, mine, length, cap,
        (factors, w_t),
    )
    last = (placed,)
    placed = placed.reshape(2, half, columns)
    other = lax.ppermute(placed[1], "dp", swap)
    factors = lax.dynamic_slice_in_dim(factors, me * part, part) + theirs
    output = jnp.where(
        me == 0, jnp.concatenate((placed[0], other)), jnp.concatenate((other, placed[0]))
    )
    grad_home = None
    for k in both:
        grad_home = input_gradient(
            pieces[k], w_t, place, low, a_t, job, length, step_blocks // 2, k, grad_home, last
        )
        last = (output,)
    return output, grad_home, factors[:, :features].T, factors[:, features:]


def local(*args):
    x, group, dy = args[0], args[1], args[7]
    size = lax.axis_size("tensor")
    blocks = group.shape[0]
    length = x.shape[0] // blocks
    fits = (
        lax.axis_size("dp") == 2
        and size % 2 == 0
        and size in (4, 8)
        and dy.shape[1] % 128 == 0
        and x.shape[1] % 128 == 0
        and length == LANES
        and args[5].shape[1] % (2 * LANES) == 0
        and blocks % 8 == 0
    )
    return ring(*args) if fits else general(*args)


def solution(mesh):
    return jax.shard_map(
        local,
        mesh=mesh,
        in_specs=(
            P(("parts", "dp"), "tensor"),
            P(("parts", "dp")),
            P(("parts", "dp")),
            P(("parts", "dp")),
            P("tensor", None),
            P("tensor", None),
            P(None, "tensor"),
            P(("parts", "dp"), "tensor"),
        ),
        out_specs=(
            P(("parts", "dp"), "tensor"),
            P(("parts", "dp"), "tensor"),
            P("tensor", ("parts", "dp")),
            P(("parts", "dp"), "tensor"),
        ),
        check_vma=False,
    )
```

```python
import functools

import jax
import jax.numpy as jnp
from jax import lax
from jax.experimental import pallas as pl
from jax.experimental.pallas import tpu as pltpu
from jax.sharding import PartitionSpec as P

ADAPTER_RANK = 16
SCALE = 2.0


def split2(v):
    high = lax.reduce_precision(v, 8, 7)
    return high.astype(jnp.bfloat16), (v - high).astype(jnp.bfloat16)


def dot32(a, b, dims):
    return lax.dot_general(a, b, (dims, ((), ())), preferred_element_type=jnp.float32)


def general(x, group, slot, job, w, a, b, dy):
    groups = lax.axis_size("dp")
    blocks = group.shape[0]
    rows, features = x.shape
    length = rows // blocks
    columns = dy.shape[1]
    cap = dy.shape[0] // length // groups
    jobs = a.shape[1] // ADAPTER_RANK
    index = group * cap + slot
    got = lax.all_to_all(
        dy.reshape(groups, cap * length, columns), "dp", split_axis=0, concat_axis=0, tiled=True
    )
    dy_home = got.reshape(groups * cap, length, columns)[index].reshape(rows, columns)
    hot = jnp.repeat(job, length)[:, None] == (
        jnp.arange(jobs * ADAPTER_RANK, dtype=jnp.int32) // ADAPTER_RANK
    )

    def of_job(terms):
        kept = jnp.where(hot, terms, 0.0).reshape(rows, jobs, ADAPTER_RANK)
        return jnp.sum(kept, axis=1).T

    def spread(sums):
        return jnp.where(hot, jnp.tile(sums.T, (1, jobs)), 0.0)

    parts = jnp.stack(
        (of_job(dot32(x, a, ((1,), (0,)))), of_job(SCALE * dot32(dy_home, b, ((1,), (1,)))))
    )
    sums = lax.psum(parts, "tensor")
    low, low_grad = spread(sums[0]), spread(sums[1])
    low_hi, low_lo = split2(low)
    grad_hi, grad_lo = split2(low_grad)
    base = lax.psum_scatter(dot32(x, w, ((1,), (0,))), "tensor", scatter_dimension=1, tiled=True)
    adapter = dot32(low_hi, b, ((1,), (0,))) + dot32(low_lo, b, ((1,), (0,)))
    out_home = (base + SCALE * adapter).astype(jnp.bfloat16)
    sent = (
        jnp.zeros((groups * cap, length, columns), jnp.bfloat16)
        .at[index]
        .set(out_home.reshape(blocks, length, columns))
    )
    output = lax.all_to_all(
        sent.reshape(groups, cap * length, columns), "dp", split_axis=0, concat_axis=0, tiled=True
    ).reshape(dy.shape)
    full = lax.all_gather(dy_home, "tensor", axis=1, tiled=True)
    grad_home = (
        dot32(full, w, ((1,), (1,)))
        + dot32(grad_hi, a, ((1,), (1,)))
        + dot32(grad_lo, a, ((1,), (1,)))
    ).astype(jnp.bfloat16)
    a_term = dot32(x, grad_hi, ((0,), (0,))) + dot32(x, grad_lo, ((0,), (0,)))
    b_term = SCALE * (dot32(low_hi, dy_home, ((0,), (0,))) + dot32(low_lo, dy_home, ((0,), (0,))))
    return (
        output,
        grad_home,
        lax.psum_scatter(a_term, "dp", scatter_dimension=1, tiled=True),
        lax.psum_scatter(b_term, "dp", scatter_dimension=0, tiled=True),
    )

RANGE = 32766.0
STEPS = 64.0
PAD = 16
VMEM_BYTES = 63 * 1024 * 1024


SMEM = pl.BlockSpec(memory_space=pltpu.SMEM)
VMEM = pl.BlockSpec(memory_space=pltpu.VMEM)
ANY = pl.BlockSpec(memory_space=pl.ANY)


def params():
    return pltpu.CompilerParams(vmem_limit_bytes=VMEM_BYTES)


def cost():
    return pl.CostEstimate(flops=1, bytes_accessed=1, transcendentals=0)


def halves(v):
    high = v.astype(jnp.bfloat16)
    return high, (v - high.astype(jnp.float32)).astype(jnp.bfloat16)


def store_coded(out_ref, at, v):
    rows = v.shape[0]
    top = jnp.maximum(jnp.max(jnp.abs(v), axis=0, keepdims=True), 1e-30)
    level = jnp.ceil(jnp.log2(top) * STEPS)
    coded = jnp.round(v * (jnp.exp2(level * (-1.0 / STEPS)) * (RANGE * 0.9999)))
    out_ref[at, pl.ds(0, rows), :] = coded.astype(jnp.int32).astype(jnp.int16)
    out_ref[at, pl.ds(rows, PAD), :] = (
        jnp.broadcast_to(level, (PAD, v.shape[1])).astype(jnp.int32).astype(jnp.int16)
    )


def load_coded(in_ref, at, first=0, rows=None):
    total = in_ref.shape[1] - PAD
    level = in_ref[at, pl.ds(total, PAD), :].astype(jnp.int32).astype(jnp.float32)[0:1, :]
    coded = in_ref[at, pl.ds(first, rows or total), :].astype(jnp.int32).astype(jnp.float32)
    return coded * (jnp.exp2(level * (1.0 / STEPS)) * (1.0 / (RANGE * 0.9999)))


LANES = 128
PACKED = LANES // ADAPTER_RANK


def lane_slot(shape):
    return lax.broadcasted_iota(jnp.int32, shape, len(shape) - 1) // ADAPTER_RANK


def pack(tile, i, values, job):
    kept = values[:, :LANES]
    for h in range(1, values.shape[1] // LANES):
        kept = jnp.where(job // PACKED == h, values[:, h * LANES : (h + 1) * LANES], kept)
    shift = lax.rem((i - lax.rem(job, PACKED) + PACKED) * ADAPTER_RANK, LANES)
    return jnp.where(lane_slot(tile.shape) == i, pltpu.roll(kept, shift, 1), tile)


def expand(tile, i, job, columns):
    place = lax.rem(job, PACKED)
    shift = lax.rem((place - i + PACKED) * ADAPTER_RANK, LANES)
    rolled = pltpu.roll(tile, shift, 1)
    rolled = jnp.where(lane_slot(tile.shape) == place, rolled, 0.0)
    return jnp.concatenate(
        [jnp.where(job // PACKED == h, rolled, 0.0) for h in range(columns // LANES)], axis=1
    )


def coded_spec(group_rows, columns):
    return pl.BlockSpec((1, group_rows + PAD, columns), lambda g, *_: (g, 0, 0))


def coded_shape(rows, group_rows, columns):
    return jax.ShapeDtypeStruct((rows // group_rows, group_rows + PAD, columns), jnp.int16)


def project(x, first, rows, w, place, offsets, received, plain, group_rows, columns, after):
    features = x.shape[1]
    count = len(offsets)
    start = first // group_rows

    def kernel(place_ref, x_ref, *refs):
        weight_ref, outs = refs[-1], refs[-1 - count : -1]

        @pl.when(pl.program_id(0) == 0)
        def _():
            for i in range(count):
                weight_ref[:, i * columns : (i + 1) * columns] = refs[i][...]

        product = dot32(x_ref[...], weight_ref[...], ((1,), (0,)))
        for i in range(count):
            part = product[:, i * columns : (i + 1) * columns]
            if i < len(received):
                part = part + load_coded(refs[count + i], 0)
            if plain and i == count - 1:
                outs[i][...] = part
            else:
                store_coded(outs[i], 0, part)

    def weight_spec(d):
        return pl.BlockSpec((features, columns), lambda g, place_ref: (0, place_ref[d]))

    coded = count - plain
    return pl.pallas_call(
        kernel,
        grid_spec=pltpu.PrefetchScalarGridSpec(
            num_scalar_prefetch=1,
            grid=(rows // group_rows,),
            in_specs=[pl.BlockSpec((group_rows, features), lambda g, place_ref: (g + start, 0))]
            + [weight_spec(d) for d in offsets]
            + [coded_spec(group_rows, columns)] * len(received)
            + [ANY] * len(after),
            out_specs=[coded_spec(group_rows, columns)] * coded
            + [pl.BlockSpec((group_rows, columns), lambda g, place_ref: (g, 0))] * plain,
            scratch_shapes=[pltpu.VMEM((features, count * columns), jnp.bfloat16)],
        ),
        out_shape=[coded_shape(rows, group_rows, columns)] * coded
        + [jax.ShapeDtypeStruct((rows, columns), jnp.float32)] * plain,
        compiler_params=params(),
        cost_estimate=cost(),
        name="project",
    )(place, x, *([w] * count), *received, *after)


def add_coded(pairs, group_rows, after, sums=False, coded=True, groups=1):
    rows, columns = pairs[0][0].shape
    count = len(pairs)

    def kernel(*refs):
        outs = refs[2 * count + len(after) :]
        for p in range(count):
            for g in range(groups):
                here = pl.ds(g * group_rows, group_rows)
                total = refs[2 * p][here, :] + load_coded(refs[2 * p + 1], g)
                if sums:
                    outs[p][here, :] = total
                if coded:
                    store_coded(outs[count * sums + p], g, total)

    block = pl.BlockSpec((groups * group_rows, columns), lambda g: (g, 0))
    coded_block = pl.BlockSpec((groups, group_rows + PAD, columns), lambda g: (g, 0, 0))
    return pl.pallas_call(
        kernel,
        grid=(rows // group_rows // groups,),
        in_specs=[block, coded_block] * count + [ANY] * len(after),
        out_specs=[block] * (count * sums) + [coded_block] * (count * coded),
        out_shape=[jax.ShapeDtypeStruct((rows, columns), jnp.float32)] * (count * sums)
        + [coded_shape(rows, group_rows, columns)] * (count * coded),
        compiler_params=params(),
        cost_estimate=cost(),
        name="add_coded",
    )(*[v for pair in pairs for v in pair], *after)


def home_gradient(dy, received, group, slot, me, length, streams, after):
    blocks = group.shape[0]
    columns = dy.shape[1]
    half = received.shape[0]
    per = blocks // streams

    def kernel(group_ref, slot_ref, me_ref, dy_ref, received_ref, *refs):
        outs = refs[len(after) :]
        mine = me_ref[0]

        def put(n, value):
            outs[0][pl.ds(n * length, length), :] = value
            outs[1 + n // per][pl.ds(n % per * length, length), :] = value

        for n in range(blocks):
            at = slot_ref[n] * length

            @pl.when(group_ref[n] == mine)
            def _():
                put(n, dy_ref[pl.ds(pl.multiple_of(mine * half + at, length), length), :])

            @pl.when(group_ref[n] != mine)
            def _():
                put(n, received_ref[pl.ds(pl.multiple_of(at, length), length), :])

    return pl.pallas_call(
        kernel,
        in_specs=[SMEM] * 3 + [VMEM] * 2 + [ANY] * len(after),
        out_specs=[VMEM] * (1 + streams),
        out_shape=[jax.ShapeDtypeStruct((blocks * length, columns), jnp.bfloat16)]
        + [jax.ShapeDtypeStruct((per * length, columns), jnp.bfloat16)] * streams,
        compiler_params=params(),
        cost_estimate=cost(),
        name="home_gradient",
    )(group, slot, me, dy, received, *after)


def low_rank(x, a, dy_home, b_t, job, length, after):
    blocks = job.shape[0]
    features = x.shape[1]
    columns = dy_home.shape[1]

    def kernel(job_ref, x_ref, a_ref, dy_ref, b_ref, *refs):
        low_ref, coded_ref = refs[-2:]
        first = pl.program_id(0) * PACKED
        products = (
            dot32(x_ref[...], a_ref[...], ((1,), (0,))),
            SCALE * dot32(dy_ref[...], b_ref[...], ((1,), (0,))),
        )
        for kind, product in enumerate(products):
            tile = jnp.zeros((length, LANES), jnp.float32)
            for i in range(PACKED):
                tile = pack(tile, i, product[i * length : (i + 1) * length], job_ref[first + i])
            low_ref[pl.ds(kind * length, length), :] = tile
            store_coded(coded_ref, kind, tile)

    rows = PACKED * length
    return pl.pallas_call(
        kernel,
        grid_spec=pltpu.PrefetchScalarGridSpec(
            num_scalar_prefetch=1,
            grid=(blocks // PACKED,),
            in_specs=[
                pl.BlockSpec((rows, features), lambda g, job_ref: (g, 0)),
                pl.BlockSpec(a.shape, lambda g, job_ref: (0, 0)),
                pl.BlockSpec((rows, columns), lambda g, job_ref: (g, 0)),
                pl.BlockSpec(b_t.shape, lambda g, job_ref: (0, 0)),
            ]
            + [ANY] * len(after),
            out_specs=[
                pl.BlockSpec((2 * length, LANES), lambda g, job_ref: (g, 0)),
                pl.BlockSpec((2, length + PAD, LANES), lambda g, job_ref: (g, 0, 0)),
            ],
        ),
        out_shape=[
            jax.ShapeDtypeStruct((blocks // PACKED * 2 * length, LANES), jnp.float32),
            coded_shape(blocks // PACKED * 2 * length, length, LANES),
        ],
        compiler_params=params(),
        cost_estimate=cost(),
        name="low_rank",
    )(job, x, a, dy_home, b_t, *after)


def factor_gradients(x, dy_home, low, job, me, ranks, length, after):
    blocks = job.shape[0]
    features = x.shape[1]
    columns = dy_home.shape[1]

    part = ranks // 2

    def kernel(job_ref, me_ref, x_ref, dy_ref, low_ref, *refs):
        kept_ref, sent_ref, out_ref = refs[-3:]
        step = pl.program_id(0)
        spread = []
        for kind in range(2):
            tile = low_ref[pl.ds(kind * length, length), :]
            wide = jnp.concatenate(
                [expand(tile, i, job_ref[step * PACKED + i], ranks) for i in range(PACKED)], axis=0
            )
            spread.append(jnp.concatenate(halves(wide), axis=1))
        down = dot32(spread[1], x_ref[...], ((0,), (0,)))
        up = SCALE * dot32(spread[0], dy_ref[...], ((0,), (0,)))

        @pl.when(step == 0)
        def _():
            out_ref[...] = jnp.zeros_like(out_ref)

        out_ref[:, pl.ds(0, features)] += down[:ranks] + down[ranks:]
        out_ref[:, pl.ds(features, columns)] += up[:ranks] + up[ranks:]

        @pl.when(step == blocks // PACKED - 1)
        def _():
            kept_ref[...] = out_ref[pl.ds(pl.multiple_of(me_ref[0] * part, part), part), :]
            sent_ref[...] = out_ref[pl.ds(pl.multiple_of((1 - me_ref[0]) * part, part), part), :]

    rows = PACKED * length
    shape = (part, features + columns)
    return pl.pallas_call(
        kernel,
        grid_spec=pltpu.PrefetchScalarGridSpec(
            num_scalar_prefetch=2,
            grid=(blocks // PACKED,),
            in_specs=[
                pl.BlockSpec((rows, features), lambda g, *_: (g, 0)),
                pl.BlockSpec((rows, columns), lambda g, *_: (g, 0)),
                pl.BlockSpec((2 * length, LANES), lambda g, *_: (g, 0)),
            ]
            + [ANY] * len(after),
            out_specs=[pl.BlockSpec(shape, lambda g, *_: (0, 0))] * 2,
            scratch_shapes=[pltpu.VMEM((ranks, features + columns), jnp.float32)],
        ),
        out_shape=[jax.ShapeDtypeStruct(shape, jnp.float32)] * 2,
        compiler_params=params(),
        cost_estimate=cost(),
        name="factor_gradients",
    )(job, me, x, dy_home, low, *after)


def place_output(own, from_left, from_right, low, b, group, slot, job, me, length, cap, after):
    blocks = group.shape[0]
    ranks, columns = b.shape
    per_group = (from_left[0].shape[1] - PAD) // length
    count = len(own)
    per_stream = blocks // count

    def kernel(group_ref, slot_ref, job_ref, me_ref, low_ref, b_ref, *refs):
        kept_ref, sent_ref = refs[-2:]
        mine = me_ref[0]
        kept_ref[...] = jnp.zeros_like(kept_ref)
        factors = jnp.concatenate((b_ref[...], b_ref[...]), axis=0)
        for n in range(blocks):
            own_ref, left_ref, right_ref = refs[3 * (n // per_stream) :][:3]
            m = n % per_stream
            g, i = m // per_group, m % per_group
            total = (
                own_ref[pl.ds(m * length, length), :]
                + load_coded(left_ref, g, i * length, length)
                + load_coded(right_ref, g, i * length, length)
            )
            tile = low_ref[pl.ds(n // PACKED * 2 * length, length), :]
            wide = jnp.concatenate(
                halves(expand(SCALE * tile, n % PACKED, job_ref[n], ranks)), axis=1
            )
            total = total + dot32(wide, factors, ((1,), (0,)))
            kept_ref[group_ref[n] * cap + slot_ref[n]] = total.astype(jnp.bfloat16)
        sent_ref[...] = kept_ref[pl.ds((1 - mine) * cap, cap)]

    sums = [v for k in range(count) for v in (own[k], from_left[k], from_right[k])]
    return pl.pallas_call(
        kernel,
        in_specs=[SMEM] * 4 + [VMEM] * (2 + len(sums)) + [ANY] * len(after),
        out_specs=[VMEM, VMEM],
        out_shape=[
            jax.ShapeDtypeStruct((2 * cap, length, columns), jnp.bfloat16),
            jax.ShapeDtypeStruct((cap, length, columns), jnp.bfloat16),
        ],
        compiler_params=params(),
        cost_estimate=cost(),
        name="place_output",
    )(group, slot, job, me, low, b, *sums, *after)


def complete(kept, received, me):
    def kernel(me_ref, received_ref, kept_ref, out_ref):
        out_ref[...] = received_ref[...]

    return pl.pallas_call(
        kernel,
        grid_spec=pltpu.PrefetchScalarGridSpec(
            num_scalar_prefetch=1,
            grid=(1,),
            in_specs=[pl.BlockSpec(received.shape, lambda g, me_ref: (0, 0, 0)), ANY],
            out_specs=pl.BlockSpec(received.shape, lambda g, me_ref: (1 - me_ref[0], 0, 0)),
        ),
        out_shape=jax.ShapeDtypeStruct(kept.shape, kept.dtype),
        input_output_aliases={2: 0},
        compiler_params=params(),
        cost_estimate=cost(),
        name="complete",
    )(me, received, kept)


def input_gradient(pieces, w_t, place, low, a_t, job, length, step_blocks, stream, after):
    offsets = sorted(pieces)
    count = len(offsets)
    stream_rows, columns = pieces[0].shape
    ranks, features = a_t.shape
    depth = count * columns + 2 * ranks
    steps = stream_rows // (step_blocks * length)
    start = stream * steps

    def kernel(job_ref, place_ref, *refs):
        weights, parts = refs[:count], refs[count : 2 * count]
        low_ref, a_ref = refs[2 * count : 2 * count + 2]
        out_ref, factor_ref = refs[-2:]

        @pl.when(pl.program_id(0) == 0)
        def _():
            for i in range(count):
                factor_ref[pl.ds(i * columns, columns), :] = weights[i][...]
            for i in range(2):
                factor_ref[pl.ds(count * columns + i * ranks, ranks), :] = a_ref[...]

        wide = []
        for i in range(step_blocks):
            n = (pl.program_id(0) + start) * step_blocks + i
            first = pl.multiple_of((2 * (n // PACKED) + 1) * length, length)
            tile = low_ref[pl.ds(first, length), :]
            wide.append(expand(tile, lax.rem(n, PACKED), job_ref[n], ranks))
        lhs = [r[...] for r in parts] + list(halves(jnp.concatenate(wide, axis=0)))
        out_ref[...] = dot32(jnp.concatenate(lhs, axis=1), factor_ref[...], ((1,), (0,)))

    step_rows = step_blocks * length

    def weight_spec(d):
        return pl.BlockSpec((columns, features), lambda g, job_ref, place_ref: (place_ref[d], 0))

    def whole_spec(v):
        return pl.BlockSpec(v.shape, lambda g, job_ref, place_ref: (0, 0))

    def row_spec(width):
        return pl.BlockSpec((step_rows, width), lambda g, job_ref, place_ref: (g, 0))

    return pl.pallas_call(
        kernel,
        grid_spec=pltpu.PrefetchScalarGridSpec(
            num_scalar_prefetch=2,
            grid=(steps,),
            in_specs=[weight_spec(d) for d in offsets]
            + [row_spec(columns)] * count
            + [whole_spec(low), whole_spec(a_t)]
            + [ANY] * len(after),
            out_specs=row_spec(features),
            scratch_shapes=[pltpu.VMEM((depth, features), jnp.bfloat16)],
        ),
        out_shape=jax.ShapeDtypeStruct((stream_rows, features), jnp.float32),
        compiler_params=params(),
        cost_estimate=cost(),
        name="input_gradient",
    )(job, place, *([w_t] * count), *[pieces[d] for d in offsets], low, a_t, *after)


def add_pieces(pieces, early, w_t, place, steps, after):
    streams = len(pieces)
    offsets = sorted(pieces[0])
    count = len(offsets)
    stream_rows, columns = early[0].shape[0], pieces[0][offsets[0]].shape[1]
    features = w_t.shape[1]
    step_rows = stream_rows // steps

    def kernel(place_ref, *refs):
        weights, parts = refs[:count], refs[count : count * (1 + streams)]
        held = refs[count * (1 + streams) :][:streams]
        out_ref, factor_ref = refs[-2:]

        @pl.when(pl.program_id(0) == 0)
        def _():
            for i in range(count):
                factor_ref[pl.ds(i * columns, columns), :] = weights[i][...]

        for k in range(streams):

            @pl.when(pl.program_id(0) // steps == k)
            def _():
                lhs = jnp.concatenate([r[...] for r in parts[k * count : (k + 1) * count]], axis=1)
                out_ref[...] = (
                    dot32(lhs, factor_ref[...], ((1,), (0,))) + held[k][...]
                ).astype(jnp.bfloat16)

    def weight_spec(d):
        return pl.BlockSpec((columns, features), lambda g, place_ref: (place_ref[d], 0))

    def row_spec(k, width):
        return pl.BlockSpec(
            (step_rows, width), lambda g, place_ref: (jnp.clip(g - k * steps, 0, steps - 1), 0)
        )

    return pl.pallas_call(
        kernel,
        grid_spec=pltpu.PrefetchScalarGridSpec(
            num_scalar_prefetch=1,
            grid=(streams * steps,),
            in_specs=[weight_spec(d) for d in offsets]
            + [row_spec(k, columns) for k in range(streams) for _ in offsets]
            + [row_spec(k, features) for k in range(streams)]
            + [ANY] * len(after),
            out_specs=pl.BlockSpec((step_rows, features), lambda g, place_ref: (g, 0)),
            scratch_shapes=[pltpu.VMEM((count * columns, features), jnp.bfloat16)],
        ),
        out_shape=jax.ShapeDtypeStruct((streams * stream_rows, features), jnp.bfloat16),
        compiler_params=params(),
        cost_estimate=cost(),
        name="add_pieces",
    )(place, *([w_t] * count), *[p[d] for p in pieces for d in offsets], *early, *after)


def ring(x, group, slot, job, w, a, b, dy):
    size = lax.axis_size("tensor")
    me = lax.axis_index("dp").astype(jnp.int32)
    blocks = group.shape[0]
    rows, features = x.shape
    length = rows // blocks
    columns = dy.shape[1]
    half = dy.shape[0] // 2
    cap = half // length
    streams = 2
    part_rows = rows // streams
    step_blocks = blocks // streams // 2
    group_rows = step_blocks * length

    order = [2 * r for r in range(size // 2)] + [2 * r + 1 for r in reversed(range(size // 2))]
    me_tensor = lax.axis_index("tensor").astype(jnp.int32)
    here = jnp.where(me_tensor % 2 == 0, me_tensor // 2, size - 1 - me_tensor // 2)
    there = (here + jnp.arange(size, dtype=jnp.int32)) % size
    place = jnp.where(there < size // 2, 2 * there, 2 * (size - 1 - there) + 1)
    ahead = [(order[r], order[(r + 1) % size]) for r in range(size)]
    back = [(order[r], order[(r - 1) % size]) for r in range(size)]
    swap = [(0, 1), (1, 0)]

    def right(v):
        return lax.ppermute(v, "tensor", ahead)

    def left(v):
        return lax.ppermute(v, "tensor", back)

    def exchange(v, bit):
        return lax.ppermute(v, "tensor", [(t, t ^ bit) for t in range(size)])

    mine = me[None]
    got = lax.ppermute(lax.dynamic_slice_in_dim(dy, (1 - me) * half, half), "dp", swap)

    far, near = size // 2, size // 2 - 1
    both = range(streams)
    ranks = a.shape[1]
    sums_r, sums_l, held_r, held_l, own, pieces = [], [], [], [], [], []

    def terms(k, offsets, received, plain, after):
        return project(
            x, k * part_rows, part_rows, w, place, offsets, received, plain, group_rows, columns, after
        )

    def first(k, after):
        r, l = terms(k, (far, size - near), (), False, after)
        sums_r.append(right(r))
        sums_l.append(left(l))
        return (r,)

    last = first(0, ())
    dy_home, *parts = home_gradient(dy, got, group, slot, mine, length, streams, last)
    for k in both:
        held_r.append(right(parts[k]))
        held_l.append(left(parts[k]))
        pieces.append({0: parts[k], size - 1: held_r[k], 1: held_l[k]})
    last = first(1, (dy_home,))
    low, coded = low_rank(x, a, dy_home, b.T, job, length, last)
    last = (coded,)
    bit = 1
    swapped = exchange(coded, bit)

    def low_step():
        nonlocal low, swapped, bit, last
        if bit >= size:
            return
        more = 2 * bit < size
        got = add_coded([(low, swapped)], length, last, True, more, low.shape[0] // length)
        low = got[0]
        last = (low,)
        bit *= 2
        if more:
            swapped = exchange(got[1], bit)

    w_t, a_t = w.T, a.T
    kept = sent = None
    for d in range(1, far):
        if d == far - 1:
            low_step()
            kept, sent = factor_gradients(
                x, dy_home, low, job, mine, ranks, length, last + (w_t, a_t)
            )
            last = (kept,)
        for k in both:
            if near > d:
                turn_r, turn_l = terms(
                    k, (far - d, size - (near - d)), (sums_r[k], sums_l[k]), False, last
                )
                sums_l[k] = left(turn_l)
            else:
                turn_r, term = terms(k, (far - d, 0), (sums_r[k],), True, last)
                own.append(term)
            sums_r[k] = right(turn_r)
            last = (turn_r, held_l[k])
            if d < near:
                last += (held_r[k],)
                held_r[k] = right(held_r[k])
                pieces[k][size - 1 - d] = held_r[k]
            held_l[k] = left(held_l[k])
            pieces[k][1 + d] = held_l[k]
            if d == 1:
                low_step()

    factors = kept + lax.ppermute(sent, "dp", swap)
    grad_a, grad_b = factors[:, :features].T, factors[:, features:]

    late = (far - 1, far)
    last = last[:1] + tuple(pieces[k][far - 1] for k in both)
    early = []
    for k in both:
        ready = {d: v for d, v in pieces[k].items() if d not in late}
        early.append(
            input_gradient(ready, w_t, place, low, a_t, job, length, step_blocks // 2, k, last)
        )
        last = (early[k], grad_a, grad_b)
    final = [{d: pieces[k][d] for d in late} for k in both]
    placed, sent = place_output(
        own, sums_r, sums_l, low, b, group, slot, job, mine, length, cap, last + tuple(pieces[k][far] for k in both)
    )
    grad_home = add_pieces(final, early, w_t, place, 2, (placed,))
    output = complete(placed, lax.ppermute(sent, "dp", swap), mine)
    return output.reshape(dy.shape), grad_home, grad_a, grad_b


def local(*args):
    x, group, dy = args[0], args[1], args[7]
    size = lax.axis_size("tensor")
    blocks = group.shape[0]
    length = x.shape[0] // blocks
    fits = (
        lax.axis_size("dp") == 2
        and size % 2 == 0
        and size in (4, 8)
        and dy.shape[1] % 128 == 0
        and x.shape[1] % 128 == 0
        and length == LANES
        and args[5].shape[1] % (2 * LANES) == 0
        and blocks % 8 == 0
    )
    return ring(*args) if fits else general(*args)


def solution(mesh):
    return jax.shard_map(
        local,
        mesh=mesh,
        in_specs=(
            P(("parts", "dp"), "tensor"),
            P(("parts", "dp")),
            P(("parts", "dp")),
            P(("parts", "dp")),
            P("tensor", None),
            P("tensor", None),
            P(None, "tensor"),
            P(("parts", "dp"), "tensor"),
        ),
        out_specs=(
            P(("parts", "dp"), "tensor"),
            P(("parts", "dp"), "tensor"),
            P("tensor", ("parts", "dp")),
            P(("parts", "dp"), "tensor"),
        ),
        check_vma=False,
    )
```

```python
import functools

import jax
import jax.numpy as jnp
from jax import lax
from jax.experimental import pallas as pl
from jax.experimental.pallas import tpu as pltpu
from jax.sharding import PartitionSpec as P

ADAPTER_RANK = 16
SCALE = 2.0


def split2(v):
    high = lax.reduce_precision(v, 8, 7)
    return high.astype(jnp.bfloat16), (v - high).astype(jnp.bfloat16)


def dot32(a, b, dims):
    return lax.dot_general(a, b, (dims, ((), ())), preferred_element_type=jnp.float32)


def general(x, group, slot, job, w, a, b, dy):
    groups = lax.axis_size("dp")
    blocks = group.shape[0]
    rows, features = x.shape
    length = rows // blocks
    columns = dy.shape[1]
    cap = dy.shape[0] // length // groups
    jobs = a.shape[1] // ADAPTER_RANK
    index = group * cap + slot
    got = lax.all_to_all(
        dy.reshape(groups, cap * length, columns), "dp", split_axis=0, concat_axis=0, tiled=True
    )
    dy_home = got.reshape(groups * cap, length, columns)[index].reshape(rows, columns)
    hot = jnp.repeat(job, length)[:, None] == (
        jnp.arange(jobs * ADAPTER_RANK, dtype=jnp.int32) // ADAPTER_RANK
    )

    def of_job(terms):
        kept = jnp.where(hot, terms, 0.0).reshape(rows, jobs, ADAPTER_RANK)
        return jnp.sum(kept, axis=1).T

    def spread(sums):
        return jnp.where(hot, jnp.tile(sums.T, (1, jobs)), 0.0)

    parts = jnp.stack(
        (of_job(dot32(x, a, ((1,), (0,)))), of_job(SCALE * dot32(dy_home, b, ((1,), (1,)))))
    )
    sums = lax.psum(parts, "tensor")
    low, low_grad = spread(sums[0]), spread(sums[1])
    low_hi, low_lo = split2(low)
    grad_hi, grad_lo = split2(low_grad)
    base = lax.psum_scatter(dot32(x, w, ((1,), (0,))), "tensor", scatter_dimension=1, tiled=True)
    adapter = dot32(low_hi, b, ((1,), (0,))) + dot32(low_lo, b, ((1,), (0,)))
    out_home = (base + SCALE * adapter).astype(jnp.bfloat16)
    sent = (
        jnp.zeros((groups * cap, length, columns), jnp.bfloat16)
        .at[index]
        .set(out_home.reshape(blocks, length, columns))
    )
    output = lax.all_to_all(
        sent.reshape(groups, cap * length, columns), "dp", split_axis=0, concat_axis=0, tiled=True
    ).reshape(dy.shape)
    full = lax.all_gather(dy_home, "tensor", axis=1, tiled=True)
    grad_home = (
        dot32(full, w, ((1,), (1,)))
        + dot32(grad_hi, a, ((1,), (1,)))
        + dot32(grad_lo, a, ((1,), (1,)))
    ).astype(jnp.bfloat16)
    a_term = dot32(x, grad_hi, ((0,), (0,))) + dot32(x, grad_lo, ((0,), (0,)))
    b_term = SCALE * (dot32(low_hi, dy_home, ((0,), (0,))) + dot32(low_lo, dy_home, ((0,), (0,))))
    return (
        output,
        grad_home,
        lax.psum_scatter(a_term, "dp", scatter_dimension=1, tiled=True),
        lax.psum_scatter(b_term, "dp", scatter_dimension=0, tiled=True),
    )

RANGE = 32766.0
STEPS = 64.0
PAD = 16
VMEM_BYTES = 63 * 1024 * 1024


SMEM = pl.BlockSpec(memory_space=pltpu.SMEM)
VMEM = pl.BlockSpec(memory_space=pltpu.VMEM)
ANY = pl.BlockSpec(memory_space=pl.ANY)


def params():
    return pltpu.CompilerParams(vmem_limit_bytes=VMEM_BYTES)


def cost():
    return pl.CostEstimate(flops=1, bytes_accessed=1, transcendentals=0)


def halves(v):
    high = v.astype(jnp.bfloat16)
    return high, (v - high.astype(jnp.float32)).astype(jnp.bfloat16)


def store_coded(out_ref, at, v):
    rows = v.shape[0]
    top = jnp.maximum(jnp.max(jnp.abs(v), axis=0, keepdims=True), 1e-30)
    level = jnp.ceil(jnp.log2(top) * STEPS)
    coded = jnp.round(v * (jnp.exp2(level * (-1.0 / STEPS)) * (RANGE * 0.9999)))
    out_ref[at, pl.ds(0, rows), :] = coded.astype(jnp.int32).astype(jnp.int16)
    out_ref[at, pl.ds(rows, PAD), :] = (
        jnp.broadcast_to(level, (PAD, v.shape[1])).astype(jnp.int32).astype(jnp.int16)
    )


def load_coded(in_ref, at, first=0, rows=None):
    total = in_ref.shape[1] - PAD
    level = in_ref[at, pl.ds(total, PAD), :].astype(jnp.int32).astype(jnp.float32)[0:1, :]
    coded = in_ref[at, pl.ds(first, rows or total), :].astype(jnp.int32).astype(jnp.float32)
    return coded * (jnp.exp2(level * (1.0 / STEPS)) * (1.0 / (RANGE * 0.9999)))


LANES = 128
PACKED = LANES // ADAPTER_RANK


def lane_slot(shape):
    return lax.broadcasted_iota(jnp.int32, shape, len(shape) - 1) // ADAPTER_RANK


def pack(tile, i, values, job):
    kept = values[:, :LANES]
    for h in range(1, values.shape[1] // LANES):
        kept = jnp.where(job // PACKED == h, values[:, h * LANES : (h + 1) * LANES], kept)
    shift = lax.rem((i - lax.rem(job, PACKED) + PACKED) * ADAPTER_RANK, LANES)
    return jnp.where(lane_slot(tile.shape) == i, pltpu.roll(kept, shift, 1), tile)


def expand(tile, i, job, columns):
    place = lax.rem(job, PACKED)
    shift = lax.rem((place - i + PACKED) * ADAPTER_RANK, LANES)
    rolled = pltpu.roll(tile, shift, 1)
    rolled = jnp.where(lane_slot(tile.shape) == place, rolled, 0.0)
    return jnp.concatenate(
        [jnp.where(job // PACKED == h, rolled, 0.0) for h in range(columns // LANES)], axis=1
    )


def coded_spec(group_rows, columns):
    return pl.BlockSpec((1, group_rows + PAD, columns), lambda g, *_: (g, 0, 0))


def coded_shape(rows, group_rows, columns):
    return jax.ShapeDtypeStruct((rows // group_rows, group_rows + PAD, columns), jnp.int16)


def project(x, first, rows, w, place, offsets, received, plain, group_rows, columns, after):
    features = x.shape[1]
    count = len(offsets)
    start = first // group_rows

    def kernel(place_ref, x_ref, *refs):
        weight_ref, outs = refs[-1], refs[-1 - count : -1]

        @pl.when(pl.program_id(0) == 0)
        def _():
            for i in range(count):
                weight_ref[:, i * columns : (i + 1) * columns] = refs[i][...]

        product = dot32(x_ref[...], weight_ref[...], ((1,), (0,)))
        for i in range(count):
            part = product[:, i * columns : (i + 1) * columns]
            if i < len(received):
                part = part + load_coded(refs[count + i], 0)
            if plain and i == count - 1:
                outs[i][...] = part
            else:
                store_coded(outs[i], 0, part)

    def weight_spec(d):
        return pl.BlockSpec((features, columns), lambda g, place_ref: (0, place_ref[d]))

    coded = count - plain
    return pl.pallas_call(
        kernel,
        grid_spec=pltpu.PrefetchScalarGridSpec(
            num_scalar_prefetch=1,
            grid=(rows // group_rows,),
            in_specs=[pl.BlockSpec((group_rows, features), lambda g, place_ref: (g + start, 0))]
            + [weight_spec(d) for d in offsets]
            + [coded_spec(group_rows, columns)] * len(received)
            + [ANY] * len(after),
            out_specs=[coded_spec(group_rows, columns)] * coded
            + [pl.BlockSpec((group_rows, columns), lambda g, place_ref: (g, 0))] * plain,
            scratch_shapes=[pltpu.VMEM((features, count * columns), jnp.bfloat16)],
        ),
        out_shape=[coded_shape(rows, group_rows, columns)] * coded
        + [jax.ShapeDtypeStruct((rows, columns), jnp.float32)] * plain,
        compiler_params=params(),
        cost_estimate=cost(),
        name="project",
    )(place, x, *([w] * count), *received, *after)


def add_coded(pairs, group_rows, after, sums=False, coded=True, groups=1):
    rows, columns = pairs[0][0].shape
    count = len(pairs)

    def kernel(*refs):
        outs = refs[2 * count + len(after) :]
        for p in range(count):
            for g in range(groups):
                here = pl.ds(g * group_rows, group_rows)
                total = refs[2 * p][here, :] + load_coded(refs[2 * p + 1], g)
                if sums:
                    outs[p][here, :] = total
                if coded:
                    store_coded(outs[count * sums + p], g, total)

    block = pl.BlockSpec((groups * group_rows, columns), lambda g: (g, 0))
    coded_block = pl.BlockSpec((groups, group_rows + PAD, columns), lambda g: (g, 0, 0))
    return pl.pallas_call(
        kernel,
        grid=(rows // group_rows // groups,),
        in_specs=[block, coded_block] * count + [ANY] * len(after),
        out_specs=[block] * (count * sums) + [coded_block] * (count * coded),
        out_shape=[jax.ShapeDtypeStruct((rows, columns), jnp.float32)] * (count * sums)
        + [coded_shape(rows, group_rows, columns)] * (count * coded),
        compiler_params=params(),
        cost_estimate=cost(),
        name="add_coded",
    )(*[v for pair in pairs for v in pair], *after)


def home_gradient(dy, received, group, slot, me, length, streams, after):
    blocks = group.shape[0]
    columns = dy.shape[1]
    half = received.shape[0]
    per = blocks // streams

    def kernel(group_ref, slot_ref, me_ref, dy_ref, received_ref, *refs):
        outs = refs[len(after) :]
        mine = me_ref[0]

        def put(n, value):
            outs[0][pl.ds(n * length, length), :] = value
            outs[1 + n // per][pl.ds(n % per * length, length), :] = value

        for n in range(blocks):
            at = slot_ref[n] * length

            @pl.when(group_ref[n] == mine)
            def _():
                put(n, dy_ref[pl.ds(pl.multiple_of(mine * half + at, length), length), :])

            @pl.when(group_ref[n] != mine)
            def _():
                put(n, received_ref[pl.ds(pl.multiple_of(at, length), length), :])

    return pl.pallas_call(
        kernel,
        in_specs=[SMEM] * 3 + [VMEM] * 2 + [ANY] * len(after),
        out_specs=[VMEM] * (1 + streams),
        out_shape=[jax.ShapeDtypeStruct((blocks * length, columns), jnp.bfloat16)]
        + [jax.ShapeDtypeStruct((per * length, columns), jnp.bfloat16)] * streams,
        compiler_params=params(),
        cost_estimate=cost(),
        name="home_gradient",
    )(group, slot, me, dy, received, *after)


def low_rank(x, a, dy_home, b_t, job, length, after):
    blocks = job.shape[0]
    features = x.shape[1]
    columns = dy_home.shape[1]

    def kernel(job_ref, x_ref, a_ref, dy_ref, b_ref, *refs):
        low_ref, coded_ref = refs[-2:]
        first = pl.program_id(0) * PACKED
        products = (
            dot32(x_ref[...], a_ref[...], ((1,), (0,))),
            SCALE * dot32(dy_ref[...], b_ref[...], ((1,), (0,))),
        )
        for kind, product in enumerate(products):
            tile = jnp.zeros((length, LANES), jnp.float32)
            for i in range(PACKED):
                tile = pack(tile, i, product[i * length : (i + 1) * length], job_ref[first + i])
            low_ref[pl.ds(kind * length, length), :] = tile
            store_coded(coded_ref, kind, tile)

    rows = PACKED * length
    return pl.pallas_call(
        kernel,
        grid_spec=pltpu.PrefetchScalarGridSpec(
            num_scalar_prefetch=1,
            grid=(blocks // PACKED,),
            in_specs=[
                pl.BlockSpec((rows, features), lambda g, job_ref: (g, 0)),
                pl.BlockSpec(a.shape, lambda g, job_ref: (0, 0)),
                pl.BlockSpec((rows, columns), lambda g, job_ref: (g, 0)),
                pl.BlockSpec(b_t.shape, lambda g, job_ref: (0, 0)),
            ]
            + [ANY] * len(after),
            out_specs=[
                pl.BlockSpec((2 * length, LANES), lambda g, job_ref: (g, 0)),
                pl.BlockSpec((2, length + PAD, LANES), lambda g, job_ref: (g, 0, 0)),
            ],
        ),
        out_shape=[
            jax.ShapeDtypeStruct((blocks // PACKED * 2 * length, LANES), jnp.float32),
            coded_shape(blocks // PACKED * 2 * length, length, LANES),
        ],
        compiler_params=params(),
        cost_estimate=cost(),
        name="low_rank",
    )(job, x, a, dy_home, b_t, *after)


def factor_gradients(x, dy_home, low, job, me, ranks, length, after):
    blocks = job.shape[0]
    features = x.shape[1]
    columns = dy_home.shape[1]

    part = ranks // 2

    def kernel(job_ref, me_ref, x_ref, dy_ref, low_ref, *refs):
        kept_ref, sent_ref, out_ref = refs[-3:]
        step = pl.program_id(0)
        spread = []
        for kind in range(2):
            tile = low_ref[pl.ds(kind * length, length), :]
            wide = jnp.concatenate(
                [expand(tile, i, job_ref[step * PACKED + i], ranks) for i in range(PACKED)], axis=0
            )
            spread.append(jnp.concatenate(halves(wide), axis=1))
        down = dot32(spread[1], x_ref[...], ((0,), (0,)))
        up = SCALE * dot32(spread[0], dy_ref[...], ((0,), (0,)))

        @pl.when(step == 0)
        def _():
            out_ref[...] = jnp.zeros_like(out_ref)

        out_ref[:, pl.ds(0, features)] += down[:ranks] + down[ranks:]
        out_ref[:, pl.ds(features, columns)] += up[:ranks] + up[ranks:]

        @pl.when(step == blocks // PACKED - 1)
        def _():
            kept_ref[...] = out_ref[pl.ds(pl.multiple_of(me_ref[0] * part, part), part), :]
            sent_ref[...] = out_ref[pl.ds(pl.multiple_of((1 - me_ref[0]) * part, part), part), :]

    rows = PACKED * length
    shape = (part, features + columns)
    return pl.pallas_call(
        kernel,
        grid_spec=pltpu.PrefetchScalarGridSpec(
            num_scalar_prefetch=2,
            grid=(blocks // PACKED,),
            in_specs=[
                pl.BlockSpec((rows, features), lambda g, *_: (g, 0)),
                pl.BlockSpec((rows, columns), lambda g, *_: (g, 0)),
                pl.BlockSpec((2 * length, LANES), lambda g, *_: (g, 0)),
            ]
            + [ANY] * len(after),
            out_specs=[pl.BlockSpec(shape, lambda g, *_: (0, 0))] * 2,
            scratch_shapes=[pltpu.VMEM((ranks, features + columns), jnp.float32)],
        ),
        out_shape=[jax.ShapeDtypeStruct(shape, jnp.float32)] * 2,
        compiler_params=params(),
        cost_estimate=cost(),
        name="factor_gradients",
    )(job, me, x, dy_home, low, *after)


def add_factors(kept, received, features, after):
    rows, width = kept.shape

    def kernel(kept_ref, received_ref, *refs):
        down_ref, up_ref = refs[len(after) :]
        total = kept_ref[...] + received_ref[...]
        down_ref[...] = total[:, :features].T
        up_ref[...] = total[:, features:]

    return pl.pallas_call(
        kernel,
        in_specs=[VMEM, VMEM] + [ANY] * len(after),
        out_specs=[VMEM, VMEM],
        out_shape=[
            jax.ShapeDtypeStruct((features, rows), jnp.float32),
            jax.ShapeDtypeStruct((rows, width - features), jnp.float32),
        ],
        compiler_params=params(),
        cost_estimate=cost(),
        name="add_factors",
    )(kept, received, *after)


def place_output(own, from_left, from_right, low, b, group, slot, job, me, length, cap, after):
    blocks = group.shape[0]
    ranks, columns = b.shape
    per_group = (from_left[0].shape[1] - PAD) // length
    count = len(own)
    per_stream = blocks // count

    def kernel(group_ref, slot_ref, job_ref, me_ref, low_ref, b_ref, *refs):
        kept_ref, sent_ref = refs[-2:]
        mine = me_ref[0]
        kept_ref[...] = jnp.zeros_like(kept_ref)
        factors = jnp.concatenate((b_ref[...], b_ref[...]), axis=0)
        for n in range(blocks):
            own_ref, left_ref, right_ref = refs[3 * (n // per_stream) :][:3]
            m = n % per_stream
            g, i = m // per_group, m % per_group
            total = (
                own_ref[pl.ds(m * length, length), :]
                + load_coded(left_ref, g, i * length, length)
                + load_coded(right_ref, g, i * length, length)
            )
            tile = low_ref[pl.ds(n // PACKED * 2 * length, length), :]
            wide = jnp.concatenate(
                halves(expand(SCALE * tile, n % PACKED, job_ref[n], ranks)), axis=1
            )
            total = total + dot32(wide, factors, ((1,), (0,)))
            kept_ref[group_ref[n] * cap + slot_ref[n]] = total.astype(jnp.bfloat16)
        sent_ref[...] = kept_ref[pl.ds((1 - mine) * cap, cap)]

    sums = [v for k in range(count) for v in (own[k], from_left[k], from_right[k])]
    return pl.pallas_call(
        kernel,
        in_specs=[SMEM] * 4 + [VMEM] * (2 + len(sums)) + [ANY] * len(after),
        out_specs=[VMEM, VMEM],
        out_shape=[
            jax.ShapeDtypeStruct((2 * cap, length, columns), jnp.bfloat16),
            jax.ShapeDtypeStruct((cap, length, columns), jnp.bfloat16),
        ],
        compiler_params=params(),
        cost_estimate=cost(),
        name="place_output",
    )(group, slot, job, me, low, b, *sums, *after)


def complete(kept, received, me):
    def kernel(me_ref, received_ref, kept_ref, out_ref):
        out_ref[...] = received_ref[...]

    return pl.pallas_call(
        kernel,
        grid_spec=pltpu.PrefetchScalarGridSpec(
            num_scalar_prefetch=1,
            grid=(1,),
            in_specs=[pl.BlockSpec(received.shape, lambda g, me_ref: (0, 0, 0)), ANY],
            out_specs=pl.BlockSpec(received.shape, lambda g, me_ref: (1 - me_ref[0], 0, 0)),
        ),
        out_shape=jax.ShapeDtypeStruct(kept.shape, kept.dtype),
        input_output_aliases={2: 0},
        compiler_params=params(),
        cost_estimate=cost(),
        name="complete",
    )(me, received, kept)


def input_gradient(pieces, w_t, place, low, a_t, job, length, step_blocks, stream, made, after):
    offsets = sorted(pieces)
    count = len(offsets)
    stream_rows, columns = pieces[0].shape
    ranks, features = a_t.shape
    depth = count * columns + 2 * ranks
    steps = stream_rows // (step_blocks * length)
    start = stream * steps
    held = () if made is None else (made,)

    def kernel(job_ref, place_ref, *refs):
        weights, parts = refs[:count], refs[count : 2 * count]
        low_ref, a_ref = refs[2 * count : 2 * count + 2]
        out_ref, factor_ref = refs[-2:]

        @pl.when(pl.program_id(0) == 0)
        def _():
            for i in range(count):
                factor_ref[pl.ds(i * columns, columns), :] = weights[i][...]
            for i in range(2):
                factor_ref[pl.ds(count * columns + i * ranks, ranks), :] = a_ref[...]

        wide = []
        for i in range(step_blocks):
            n = (pl.program_id(0) + start) * step_blocks + i
            first = pl.multiple_of((2 * (n // PACKED) + 1) * length, length)
            tile = low_ref[pl.ds(first, length), :]
            wide.append(expand(tile, lax.rem(n, PACKED), job_ref[n], ranks))
        lhs = [r[...] for r in parts] + list(halves(jnp.concatenate(wide, axis=0)))
        out_ref[...] = dot32(jnp.concatenate(lhs, axis=1), factor_ref[...], ((1,), (0,)))

    step_rows = step_blocks * length

    def weight_spec(d):
        return pl.BlockSpec((columns, features), lambda g, job_ref, place_ref: (place_ref[d], 0))

    def whole_spec(v):
        return pl.BlockSpec(v.shape, lambda g, job_ref, place_ref: (0, 0))

    def row_spec(width):
        return pl.BlockSpec((step_rows, width), lambda g, job_ref, place_ref: (g, 0))

    return pl.pallas_call(
        kernel,
        grid_spec=pltpu.PrefetchScalarGridSpec(
            num_scalar_prefetch=2,
            grid=(steps,),
            in_specs=[weight_spec(d) for d in offsets]
            + [row_spec(columns)] * count
            + [whole_spec(low), whole_spec(a_t)]
            + [ANY] * (len(held) + len(after)),
            out_specs=pl.BlockSpec(
                (step_rows, features), lambda g, job_ref, place_ref: (g + start, 0)
            ),
            scratch_shapes=[pltpu.VMEM((depth, features), jnp.bfloat16)],
        ),
        out_shape=jax.ShapeDtypeStruct((job.shape[0] * length, features), jnp.float32),
        input_output_aliases={2 * count + 4: 0} if held else {},
        compiler_params=params(),
        cost_estimate=cost(),
        name="input_gradient",
    )(job, place, *([w_t] * count), *[pieces[d] for d in offsets], low, a_t, *held, *after)


def add_pieces(pieces, early, w_t, place, steps, after):
    streams = len(pieces)
    offsets = sorted(pieces[0])
    count = len(offsets)
    stream_rows, columns = pieces[0][offsets[0]].shape
    features = w_t.shape[1]
    step_rows = stream_rows // steps

    def kernel(place_ref, *refs):
        weights, parts = refs[:count], refs[count : count * (1 + streams)]
        early_ref = refs[count * (1 + streams)]
        out_ref, factor_ref = refs[-2:]

        @pl.when(pl.program_id(0) == 0)
        def _():
            for i in range(count):
                factor_ref[pl.ds(i * columns, columns), :] = weights[i][...]

        for k in range(streams):

            @pl.when(pl.program_id(0) // steps == k)
            def _():
                lhs = jnp.concatenate([r[...] for r in parts[k * count : (k + 1) * count]], axis=1)
                out_ref[...] = (
                    dot32(lhs, factor_ref[...], ((1,), (0,))) + early_ref[...]
                ).astype(jnp.bfloat16)

    def weight_spec(d):
        return pl.BlockSpec((columns, features), lambda g, place_ref: (place_ref[d], 0))

    def row_spec(k, width):
        return pl.BlockSpec(
            (step_rows, width), lambda g, place_ref: (jnp.clip(g - k * steps, 0, steps - 1), 0)
        )

    return pl.pallas_call(
        kernel,
        grid_spec=pltpu.PrefetchScalarGridSpec(
            num_scalar_prefetch=1,
            grid=(streams * steps,),
            in_specs=[weight_spec(d) for d in offsets]
            + [row_spec(k, columns) for k in range(streams) for _ in offsets]
            + [pl.BlockSpec((step_rows, features), lambda g, place_ref: (g, 0))]
            + [ANY] * len(after),
            out_specs=pl.BlockSpec((step_rows, features), lambda g, place_ref: (g, 0)),
            scratch_shapes=[pltpu.VMEM((count * columns, features), jnp.bfloat16)],
        ),
        out_shape=jax.ShapeDtypeStruct((streams * stream_rows, features), jnp.bfloat16),
        compiler_params=params(),
        cost_estimate=cost(),
        name="add_pieces",
    )(place, *([w_t] * count), *[p[d] for p in pieces for d in offsets], early, *after)


def ring(x, group, slot, job, w, a, b, dy):
    size = lax.axis_size("tensor")
    me = lax.axis_index("dp").astype(jnp.int32)
    blocks = group.shape[0]
    rows, features = x.shape
    length = rows // blocks
    columns = dy.shape[1]
    half = dy.shape[0] // 2
    cap = half // length
    streams = 2
    part_rows = rows // streams
    step_blocks = blocks // streams // 2
    group_rows = step_blocks * length

    order = [2 * r for r in range(size // 2)] + [2 * r + 1 for r in reversed(range(size // 2))]
    me_tensor = lax.axis_index("tensor").astype(jnp.int32)
    here = jnp.where(me_tensor % 2 == 0, me_tensor // 2, size - 1 - me_tensor // 2)
    there = (here + jnp.arange(size, dtype=jnp.int32)) % size
    place = jnp.where(there < size // 2, 2 * there, 2 * (size - 1 - there) + 1)
    ahead = [(order[r], order[(r + 1) % size]) for r in range(size)]
    back = [(order[r], order[(r - 1) % size]) for r in range(size)]
    swap = [(0, 1), (1, 0)]

    def right(v):
        return lax.ppermute(v, "tensor", ahead)

    def left(v):
        return lax.ppermute(v, "tensor", back)

    def exchange(v, bit):
        return lax.ppermute(v, "tensor", [(t, t ^ bit) for t in range(size)])

    mine = me[None]
    got = lax.ppermute(lax.dynamic_slice_in_dim(dy, (1 - me) * half, half), "dp", swap)

    far, near = size // 2, size // 2 - 1
    both = range(streams)
    ranks = a.shape[1]
    sums_r, sums_l, held_r, held_l, own, pieces = [], [], [], [], [], []

    def terms(k, offsets, received, plain, after):
        return project(
            x, k * part_rows, part_rows, w, place, offsets, received, plain, group_rows, columns, after
        )

    def first(k, after):
        r, l = terms(k, (far, size - near), (), False, after)
        sums_r.append(right(r))
        sums_l.append(left(l))
        return (r,)

    last = first(0, ())
    last = first(1, last)
    dy_home, *parts = home_gradient(dy, got, group, slot, mine, length, streams, last)
    for k in both:
        held_r.append(right(parts[k]))
        held_l.append(left(parts[k]))
        pieces.append({0: parts[k], size - 1: held_r[k], 1: held_l[k]})
    last = (dy_home,)
    low, coded = low_rank(x, a, dy_home, b.T, job, length, last)
    last = (coded,)
    bit = 1
    swapped = exchange(coded, bit)

    def low_step():
        nonlocal low, swapped, bit, last
        if bit >= size:
            return
        more = 2 * bit < size
        got = add_coded([(low, swapped)], length, last, True, more, low.shape[0] // length)
        low = got[0]
        last = (low,)
        bit *= 2
        if more:
            swapped = exchange(got[1], bit)

    w_t, a_t = w.T, a.T
    kept = sent = None
    for d in range(1, far):
        if d == far - 1:
            while bit < size:
                low_step()
            kept, sent = factor_gradients(
                x, dy_home, low, job, mine, ranks, length, last + (w_t, a_t)
            )
            last = (kept,)
        for k in both:
            if near > d:
                turn_r, turn_l = terms(
                    k, (far - d, size - (near - d)), (sums_r[k], sums_l[k]), False, last
                )
                sums_l[k] = left(turn_l)
            else:
                turn_r, term = terms(k, (far - d, 0), (sums_r[k],), True, last)
                own.append(term)
            sums_r[k] = right(turn_r)
            last = (turn_r, held_l[k])
            if d < near:
                last += (held_r[k],)
                held_r[k] = right(held_r[k])
                pieces[k][size - 1 - d] = held_r[k]
            held_l[k] = left(held_l[k])
            pieces[k][1 + d] = held_l[k]
            if d + k == 2:
                low_step()

    grad_a, grad_b = add_factors(kept, lax.ppermute(sent, "dp", swap), features, last[:1])

    late = (far - 1, far)
    last = last[:1] + tuple(pieces[k][far - 1] for k in both)
    early = None
    for k in both:
        ready = {d: v for d, v in pieces[k].items() if d not in late}
        early = input_gradient(
            ready, w_t, place, low, a_t, job, length, step_blocks // 2, k, early, last
        )
        last = (grad_b,)
    final = [{d: pieces[k][d] for d in late} for k in both]
    placed, sent = place_output(
        own, sums_r, sums_l, low, b, group, slot, job, mine, length, cap, (early,) + tuple(pieces[k][far] for k in both)
    )
    grad_home = add_pieces(final, early, w_t, place, 2, (placed,))
    output = complete(placed, lax.ppermute(sent, "dp", swap), mine)
    return output.reshape(dy.shape), grad_home, grad_a, grad_b


def local(*args):
    x, group, dy = args[0], args[1], args[7]
    size = lax.axis_size("tensor")
    blocks = group.shape[0]
    length = x.shape[0] // blocks
    fits = (
        lax.axis_size("dp") == 2
        and size % 2 == 0
        and size in (4, 8)
        and dy.shape[1] % 128 == 0
        and x.shape[1] % 128 == 0
        and length == LANES
        and args[5].shape[1] % (2 * LANES) == 0
        and blocks % 8 == 0
    )
    return ring(*args) if fits else general(*args)


def solution(mesh):
    return jax.shard_map(
        local,
        mesh=mesh,
        in_specs=(
            P(("parts", "dp"), "tensor"),
            P(("parts", "dp")),
            P(("parts", "dp")),
            P(("parts", "dp")),
            P("tensor", None),
            P("tensor", None),
            P(None, "tensor"),
            P(("parts", "dp"), "tensor"),
        ),
        out_specs=(
            P(("parts", "dp"), "tensor"),
            P(("parts", "dp"), "tensor"),
            P("tensor", ("parts", "dp")),
            P(("parts", "dp"), "tensor"),
        ),
        check_vma=False,
    )
```

```python
import functools

import jax
import jax.numpy as jnp
from jax import lax
from jax.experimental import pallas as pl
from jax.experimental.pallas import tpu as pltpu
from jax.sharding import PartitionSpec as P

ADAPTER_RANK = 16
SCALE = 2.0


def split2(v):
    high = lax.reduce_precision(v, 8, 7)
    return high.astype(jnp.bfloat16), (v - high).astype(jnp.bfloat16)


def dot32(a, b, dims):
    return lax.dot_general(a, b, (dims, ((), ())), preferred_element_type=jnp.float32)


def general(x, group, slot, job, w, a, b, dy):
    groups = lax.axis_size("dp")
    blocks = group.shape[0]
    rows, features = x.shape
    length = rows // blocks
    columns = dy.shape[1]
    cap = dy.shape[0] // length // groups
    jobs = a.shape[1] // ADAPTER_RANK
    index = group * cap + slot
    got = lax.all_to_all(
        dy.reshape(groups, cap * length, columns), "dp", split_axis=0, concat_axis=0, tiled=True
    )
    dy_home = got.reshape(groups * cap, length, columns)[index].reshape(rows, columns)
    hot = jnp.repeat(job, length)[:, None] == (
        jnp.arange(jobs * ADAPTER_RANK, dtype=jnp.int32) // ADAPTER_RANK
    )

    def of_job(terms):
        kept = jnp.where(hot, terms, 0.0).reshape(rows, jobs, ADAPTER_RANK)
        return jnp.sum(kept, axis=1).T

    def spread(sums):
        return jnp.where(hot, jnp.tile(sums.T, (1, jobs)), 0.0)

    parts = jnp.stack(
        (of_job(dot32(x, a, ((1,), (0,)))), of_job(SCALE * dot32(dy_home, b, ((1,), (1,)))))
    )
    sums = lax.psum(parts, "tensor")
    low, low_grad = spread(sums[0]), spread(sums[1])
    low_hi, low_lo = split2(low)
    grad_hi, grad_lo = split2(low_grad)
    base = lax.psum_scatter(dot32(x, w, ((1,), (0,))), "tensor", scatter_dimension=1, tiled=True)
    adapter = dot32(low_hi, b, ((1,), (0,))) + dot32(low_lo, b, ((1,), (0,)))
    out_home = (base + SCALE * adapter).astype(jnp.bfloat16)
    sent = (
        jnp.zeros((groups * cap, length, columns), jnp.bfloat16)
        .at[index]
        .set(out_home.reshape(blocks, length, columns))
    )
    output = lax.all_to_all(
        sent.reshape(groups, cap * length, columns), "dp", split_axis=0, concat_axis=0, tiled=True
    ).reshape(dy.shape)
    full = lax.all_gather(dy_home, "tensor", axis=1, tiled=True)
    grad_home = (
        dot32(full, w, ((1,), (1,)))
        + dot32(grad_hi, a, ((1,), (1,)))
        + dot32(grad_lo, a, ((1,), (1,)))
    ).astype(jnp.bfloat16)
    a_term = dot32(x, grad_hi, ((0,), (0,))) + dot32(x, grad_lo, ((0,), (0,)))
    b_term = SCALE * (dot32(low_hi, dy_home, ((0,), (0,))) + dot32(low_lo, dy_home, ((0,), (0,))))
    return (
        output,
        grad_home,
        lax.psum_scatter(a_term, "dp", scatter_dimension=1, tiled=True),
        lax.psum_scatter(b_term, "dp", scatter_dimension=0, tiled=True),
    )

RANGE = 32766.0
STEPS = 64.0
PAD = 16
VMEM_BYTES = 63 * 1024 * 1024


SMEM = pl.BlockSpec(memory_space=pltpu.SMEM)
VMEM = pl.BlockSpec(memory_space=pltpu.VMEM)
ANY = pl.BlockSpec(memory_space=pl.ANY)


def params():
    return pltpu.CompilerParams(vmem_limit_bytes=VMEM_BYTES)


def cost():
    return pl.CostEstimate(flops=1, bytes_accessed=1, transcendentals=0)


def halves(v):
    high = v.astype(jnp.bfloat16)
    return high, (v - high.astype(jnp.float32)).astype(jnp.bfloat16)


def store_coded(out_ref, at, v):
    rows = v.shape[0]
    top = jnp.maximum(jnp.max(jnp.abs(v), axis=0, keepdims=True), 1e-30)
    level = jnp.ceil(jnp.log2(top) * STEPS)
    coded = jnp.round(v * (jnp.exp2(level * (-1.0 / STEPS)) * (RANGE * 0.9999)))
    out_ref[at, pl.ds(0, rows), :] = coded.astype(jnp.int32).astype(jnp.int16)
    out_ref[at, pl.ds(rows, PAD), :] = (
        jnp.broadcast_to(level, (PAD, v.shape[1])).astype(jnp.int32).astype(jnp.int16)
    )


def load_coded(in_ref, at, first=0, rows=None):
    total = in_ref.shape[1] - PAD
    level = in_ref[at, pl.ds(total, PAD), :].astype(jnp.int32).astype(jnp.float32)[0:1, :]
    coded = in_ref[at, pl.ds(first, rows or total), :].astype(jnp.int32).astype(jnp.float32)
    return coded * (jnp.exp2(level * (1.0 / STEPS)) * (1.0 / (RANGE * 0.9999)))


LANES = 128
PACKED = LANES // ADAPTER_RANK


def lane_slot(shape):
    return lax.broadcasted_iota(jnp.int32, shape, len(shape) - 1) // ADAPTER_RANK


def pack(tile, i, values, job):
    kept = values[:, :LANES]
    for h in range(1, values.shape[1] // LANES):
        kept = jnp.where(job // PACKED == h, values[:, h * LANES : (h + 1) * LANES], kept)
    shift = lax.rem((i - lax.rem(job, PACKED) + PACKED) * ADAPTER_RANK, LANES)
    return jnp.where(lane_slot(tile.shape) == i, pltpu.roll(kept, shift, 1), tile)


def expand(tile, i, job, columns):
    place = lax.rem(job, PACKED)
    shift = lax.rem((place - i + PACKED) * ADAPTER_RANK, LANES)
    rolled = pltpu.roll(tile, shift, 1)
    rolled = jnp.where(lane_slot(tile.shape) == place, rolled, 0.0)
    return jnp.concatenate(
        [jnp.where(job // PACKED == h, rolled, 0.0) for h in range(columns // LANES)], axis=1
    )


def coded_spec(group_rows, columns):
    return pl.BlockSpec((1, group_rows + PAD, columns), lambda g, *_: (g, 0, 0))


def coded_shape(rows, group_rows, columns):
    return jax.ShapeDtypeStruct((rows // group_rows, group_rows + PAD, columns), jnp.int16)


def project(x, first, rows, w, place, offsets, received, plain, group_rows, columns, after):
    features = x.shape[1]
    count = len(offsets)
    start = first // group_rows

    def kernel(place_ref, x_ref, *refs):
        weight_ref, outs = refs[-1], refs[-1 - count : -1]

        @pl.when(pl.program_id(0) == 0)
        def _():
            for i in range(count):
                weight_ref[:, i * columns : (i + 1) * columns] = refs[i][...]

        product = dot32(x_ref[...], weight_ref[...], ((1,), (0,)))
        for i in range(count):
            part = product[:, i * columns : (i + 1) * columns]
            if i < len(received):
                part = part + load_coded(refs[count + i], 0)
            if plain and i == count - 1:
                outs[i][...] = part
            else:
                store_coded(outs[i], 0, part)

    def weight_spec(d):
        return pl.BlockSpec((features, columns), lambda g, place_ref: (0, place_ref[d]))

    coded = count - plain
    return pl.pallas_call(
        kernel,
        grid_spec=pltpu.PrefetchScalarGridSpec(
            num_scalar_prefetch=1,
            grid=(rows // group_rows,),
            in_specs=[pl.BlockSpec((group_rows, features), lambda g, place_ref: (g + start, 0))]
            + [weight_spec(d) for d in offsets]
            + [coded_spec(group_rows, columns)] * len(received)
            + [ANY] * len(after),
            out_specs=[coded_spec(group_rows, columns)] * coded
            + [pl.BlockSpec((group_rows, columns), lambda g, place_ref: (g, 0))] * plain,
            scratch_shapes=[pltpu.VMEM((features, count * columns), jnp.bfloat16)],
        ),
        out_shape=[coded_shape(rows, group_rows, columns)] * coded
        + [jax.ShapeDtypeStruct((rows, columns), jnp.float32)] * plain,
        compiler_params=params(),
        cost_estimate=cost(),
        name="project",
    )(place, x, *([w] * count), *received, *after)


def add_coded(pairs, group_rows, after, sums=False, coded=True, groups=1):
    rows, columns = pairs[0][0].shape
    count = len(pairs)

    def kernel(*refs):
        outs = refs[2 * count + len(after) :]
        for p in range(count):
            for g in range(groups):
                here = pl.ds(g * group_rows, group_rows)
                total = refs[2 * p][here, :] + load_coded(refs[2 * p + 1], g)
                if sums:
                    outs[p][here, :] = total
                if coded:
                    store_coded(outs[count * sums + p], g, total)

    block = pl.BlockSpec((groups * group_rows, columns), lambda g: (g, 0))
    coded_block = pl.BlockSpec((groups, group_rows + PAD, columns), lambda g: (g, 0, 0))
    return pl.pallas_call(
        kernel,
        grid=(rows // group_rows // groups,),
        in_specs=[block, coded_block] * count + [ANY] * len(after),
        out_specs=[block] * (count * sums) + [coded_block] * (count * coded),
        out_shape=[jax.ShapeDtypeStruct((rows, columns), jnp.float32)] * (count * sums)
        + [coded_shape(rows, group_rows, columns)] * (count * coded),
        compiler_params=params(),
        cost_estimate=cost(),
        name="add_coded",
    )(*[v for pair in pairs for v in pair], *after)


def home_gradient(dy, received, group, slot, me, length, streams, after):
    blocks = group.shape[0]
    columns = dy.shape[1]
    half = received.shape[0]
    per = blocks // streams

    def kernel(group_ref, slot_ref, me_ref, dy_ref, received_ref, *refs):
        outs = refs[len(after) :]
        mine = me_ref[0]

        def put(n, value):
            outs[0][pl.ds(n * length, length), :] = value
            outs[1 + n // per][pl.ds(n % per * length, length), :] = value

        for n in range(blocks):
            at = slot_ref[n] * length

            @pl.when(group_ref[n] == mine)
            def _():
                put(n, dy_ref[pl.ds(pl.multiple_of(mine * half + at, length), length), :])

            @pl.when(group_ref[n] != mine)
            def _():
                put(n, received_ref[pl.ds(pl.multiple_of(at, length), length), :])

    return pl.pallas_call(
        kernel,
        in_specs=[SMEM] * 3 + [VMEM] * 2 + [ANY] * len(after),
        out_specs=[VMEM] * (1 + streams),
        out_shape=[jax.ShapeDtypeStruct((blocks * length, columns), jnp.bfloat16)]
        + [jax.ShapeDtypeStruct((per * length, columns), jnp.bfloat16)] * streams,
        compiler_params=params(),
        cost_estimate=cost(),
        name="home_gradient",
    )(group, slot, me, dy, received, *after)


def low_rank(x, a, dy_home, b_t, job, length, after):
    blocks = job.shape[0]
    features = x.shape[1]
    columns = dy_home.shape[1]

    def kernel(job_ref, x_ref, a_ref, dy_ref, b_ref, *refs):
        low_ref, coded_ref = refs[-2:]
        first = pl.program_id(0) * PACKED
        products = (
            dot32(x_ref[...], a_ref[...], ((1,), (0,))),
            SCALE * dot32(dy_ref[...], b_ref[...], ((1,), (0,))),
        )
        for kind, product in enumerate(products):
            tile = jnp.zeros((length, LANES), jnp.float32)
            for i in range(PACKED):
                tile = pack(tile, i, product[i * length : (i + 1) * length], job_ref[first + i])
            low_ref[pl.ds(kind * length, length), :] = tile
            store_coded(coded_ref, kind, tile)

    rows = PACKED * length
    return pl.pallas_call(
        kernel,
        grid_spec=pltpu.PrefetchScalarGridSpec(
            num_scalar_prefetch=1,
            grid=(blocks // PACKED,),
            in_specs=[
                pl.BlockSpec((rows, features), lambda g, job_ref: (g, 0)),
                pl.BlockSpec(a.shape, lambda g, job_ref: (0, 0)),
                pl.BlockSpec((rows, columns), lambda g, job_ref: (g, 0)),
                pl.BlockSpec(b_t.shape, lambda g, job_ref: (0, 0)),
            ]
            + [ANY] * len(after),
            out_specs=[
                pl.BlockSpec((2 * length, LANES), lambda g, job_ref: (g, 0)),
                pl.BlockSpec((2, length + PAD, LANES), lambda g, job_ref: (g, 0, 0)),
            ],
        ),
        out_shape=[
            jax.ShapeDtypeStruct((blocks // PACKED * 2 * length, LANES), jnp.float32),
            coded_shape(blocks // PACKED * 2 * length, length, LANES),
        ],
        compiler_params=params(),
        cost_estimate=cost(),
        name="low_rank",
    )(job, x, a, dy_home, b_t, *after)


def factor_gradients(x, dy_home, low, job, me, ranks, length, after):
    blocks = job.shape[0]
    features = x.shape[1]
    columns = dy_home.shape[1]

    part = ranks // 2

    def kernel(job_ref, me_ref, x_ref, dy_ref, low_ref, *refs):
        kept_ref, sent_ref, out_ref = refs[-3:]
        step = pl.program_id(0)
        spread = []
        for kind in range(2):
            tile = low_ref[pl.ds(kind * length, length), :]
            wide = jnp.concatenate(
                [expand(tile, i, job_ref[step * PACKED + i], ranks) for i in range(PACKED)], axis=0
            )
            spread.append(jnp.concatenate(halves(wide), axis=1))
        down = dot32(spread[1], x_ref[...], ((0,), (0,)))
        up = SCALE * dot32(spread[0], dy_ref[...], ((0,), (0,)))

        @pl.when(step == 0)
        def _():
            out_ref[...] = jnp.zeros_like(out_ref)

        out_ref[:, pl.ds(0, features)] += down[:ranks] + down[ranks:]
        out_ref[:, pl.ds(features, columns)] += up[:ranks] + up[ranks:]

        @pl.when(step == blocks // PACKED - 1)
        def _():
            kept_ref[...] = out_ref[pl.ds(pl.multiple_of(me_ref[0] * part, part), part), :]
            sent_ref[...] = out_ref[pl.ds(pl.multiple_of((1 - me_ref[0]) * part, part), part), :]

    rows = PACKED * length
    shape = (part, features + columns)
    return pl.pallas_call(
        kernel,
        grid_spec=pltpu.PrefetchScalarGridSpec(
            num_scalar_prefetch=2,
            grid=(blocks // PACKED,),
            in_specs=[
                pl.BlockSpec((rows, features), lambda g, *_: (g, 0)),
                pl.BlockSpec((rows, columns), lambda g, *_: (g, 0)),
                pl.BlockSpec((2 * length, LANES), lambda g, *_: (g, 0)),
            ]
            + [ANY] * len(after),
            out_specs=[pl.BlockSpec(shape, lambda g, *_: (0, 0))] * 2,
            scratch_shapes=[pltpu.VMEM((ranks, features + columns), jnp.float32)],
        ),
        out_shape=[jax.ShapeDtypeStruct(shape, jnp.float32)] * 2,
        compiler_params=params(),
        cost_estimate=cost(),
        name="factor_gradients",
    )(job, me, x, dy_home, low, *after)


def add_factors(kept, received, features, after):
    rows, width = kept.shape

    def kernel(kept_ref, received_ref, *refs):
        down_ref, up_ref = refs[len(after) :]
        total = kept_ref[...] + received_ref[...]
        down_ref[...] = total[:, :features].T
        up_ref[...] = total[:, features:]

    return pl.pallas_call(
        kernel,
        in_specs=[VMEM, VMEM] + [ANY] * len(after),
        out_specs=[VMEM, VMEM],
        out_shape=[
            jax.ShapeDtypeStruct((features, rows), jnp.float32),
            jax.ShapeDtypeStruct((rows, width - features), jnp.float32),
        ],
        compiler_params=params(),
        cost_estimate=cost(),
        name="add_factors",
    )(kept, received, *after)


def place_output(own, from_left, from_right, low, b, group, slot, job, me, length, cap, after):
    blocks = group.shape[0]
    ranks, columns = b.shape
    per_group = (from_left[0].shape[1] - PAD) // length
    count = len(own)
    per_stream = blocks // count

    def kernel(group_ref, slot_ref, job_ref, me_ref, low_ref, b_ref, *refs):
        kept_ref, sent_ref = refs[-2:]
        mine = me_ref[0]
        kept_ref[...] = jnp.zeros_like(kept_ref)
        factors = jnp.concatenate((b_ref[...], b_ref[...]), axis=0)
        for n in range(blocks):
            own_ref, left_ref, right_ref = refs[3 * (n // per_stream) :][:3]
            m = n % per_stream
            g, i = m // per_group, m % per_group
            total = (
                own_ref[pl.ds(m * length, length), :]
                + load_coded(left_ref, g, i * length, length)
                + load_coded(right_ref, g, i * length, length)
            )
            tile = low_ref[pl.ds(n // PACKED * 2 * length, length), :]
            wide = jnp.concatenate(
                halves(expand(SCALE * tile, n % PACKED, job_ref[n], ranks)), axis=1
            )
            total = total + dot32(wide, factors, ((1,), (0,)))
            kept_ref[group_ref[n] * cap + slot_ref[n]] = total.astype(jnp.bfloat16)
        sent_ref[...] = kept_ref[pl.ds((1 - mine) * cap, cap)]

    sums = [v for k in range(count) for v in (own[k], from_left[k], from_right[k])]
    return pl.pallas_call(
        kernel,
        in_specs=[SMEM] * 4 + [VMEM] * (2 + len(sums)) + [ANY] * len(after),
        out_specs=[VMEM, VMEM],
        out_shape=[
            jax.ShapeDtypeStruct((2 * cap, length, columns), jnp.bfloat16),
            jax.ShapeDtypeStruct((cap, length, columns), jnp.bfloat16),
        ],
        compiler_params=params(),
        cost_estimate=cost(),
        name="place_output",
    )(group, slot, job, me, low, b, *sums, *after)


def complete(kept, received, me):
    def kernel(me_ref, received_ref, kept_ref, out_ref):
        out_ref[...] = received_ref[...]

    return pl.pallas_call(
        kernel,
        grid_spec=pltpu.PrefetchScalarGridSpec(
            num_scalar_prefetch=1,
            grid=(1,),
            in_specs=[pl.BlockSpec(received.shape, lambda g, me_ref: (0, 0, 0)), ANY],
            out_specs=pl.BlockSpec(received.shape, lambda g, me_ref: (1 - me_ref[0], 0, 0)),
        ),
        out_shape=jax.ShapeDtypeStruct(kept.shape, kept.dtype),
        input_output_aliases={2: 0},
        compiler_params=params(),
        cost_estimate=cost(),
        name="complete",
    )(me, received, kept)


def input_gradient(pieces, w_t, place, low, a_t, job, length, step_blocks, stream, made, after):
    offsets = sorted(pieces)
    count = len(offsets)
    stream_rows, columns = pieces[0].shape
    ranks, features = a_t.shape
    depth = count * columns + 2 * ranks
    steps = stream_rows // (step_blocks * length)
    start = stream * steps
    held = () if made is None else (made,)

    def kernel(job_ref, place_ref, *refs):
        weights, parts = refs[:count], refs[count : 2 * count]
        low_ref, a_ref = refs[2 * count : 2 * count + 2]
        out_ref, factor_ref = refs[-2:]

        @pl.when(pl.program_id(0) == 0)
        def _():
            for i in range(count):
                factor_ref[pl.ds(i * columns, columns), :] = weights[i][...]
            for i in range(2):
                factor_ref[pl.ds(count * columns + i * ranks, ranks), :] = a_ref[...]

        wide = []
        for i in range(step_blocks):
            n = (pl.program_id(0) + start) * step_blocks + i
            first = pl.multiple_of((2 * (n // PACKED) + 1) * length, length)
            tile = low_ref[pl.ds(first, length), :]
            wide.append(expand(tile, lax.rem(n, PACKED), job_ref[n], ranks))
        lhs = [r[...] for r in parts] + list(halves(jnp.concatenate(wide, axis=0)))
        out_ref[...] = dot32(jnp.concatenate(lhs, axis=1), factor_ref[...], ((1,), (0,)))

    step_rows = step_blocks * length

    def weight_spec(d):
        return pl.BlockSpec((columns, features), lambda g, job_ref, place_ref: (place_ref[d], 0))

    def whole_spec(v):
        return pl.BlockSpec(v.shape, lambda g, job_ref, place_ref: (0, 0))

    def row_spec(width):
        return pl.BlockSpec((step_rows, width), lambda g, job_ref, place_ref: (g, 0))

    return pl.pallas_call(
        kernel,
        grid_spec=pltpu.PrefetchScalarGridSpec(
            num_scalar_prefetch=2,
            grid=(steps,),
            in_specs=[weight_spec(d) for d in offsets]
            + [row_spec(columns)] * count
            + [whole_spec(low), whole_spec(a_t)]
            + [ANY] * (len(held) + len(after)),
            out_specs=pl.BlockSpec(
                (step_rows, features), lambda g, job_ref, place_ref: (g + start, 0)
            ),
            scratch_shapes=[pltpu.VMEM((depth, features), jnp.bfloat16)],
        ),
        out_shape=jax.ShapeDtypeStruct((job.shape[0] * length, features), jnp.float32),
        input_output_aliases={2 * count + 4: 0} if held else {},
        compiler_params=params(),
        cost_estimate=cost(),
        name="input_gradient",
    )(job, place, *([w_t] * count), *[pieces[d] for d in offsets], low, a_t, *held, *after)


def add_pieces(pieces, early, w_t, place, steps, after):
    streams = len(pieces)
    offsets = sorted(pieces[0])
    count = len(offsets)
    stream_rows, columns = pieces[0][offsets[0]].shape
    features = w_t.shape[1]
    step_rows = stream_rows // steps

    def kernel(place_ref, *refs):
        weights, parts = refs[:count], refs[count : count * (1 + streams)]
        early_ref = refs[count * (1 + streams)]
        out_ref, factor_ref = refs[-2:]

        @pl.when(pl.program_id(0) == 0)
        def _():
            for i in range(count):
                factor_ref[pl.ds(i * columns, columns), :] = weights[i][...]

        for k in range(streams):

            @pl.when(pl.program_id(0) // steps == k)
            def _():
                lhs = jnp.concatenate([r[...] for r in parts[k * count : (k + 1) * count]], axis=1)
                out_ref[...] = (
                    dot32(lhs, factor_ref[...], ((1,), (0,))) + early_ref[...]
                ).astype(jnp.bfloat16)

    def weight_spec(d):
        return pl.BlockSpec((columns, features), lambda g, place_ref: (place_ref[d], 0))

    def row_spec(k, width):
        return pl.BlockSpec(
            (step_rows, width), lambda g, place_ref: (jnp.clip(g - k * steps, 0, steps - 1), 0)
        )

    return pl.pallas_call(
        kernel,
        grid_spec=pltpu.PrefetchScalarGridSpec(
            num_scalar_prefetch=1,
            grid=(streams * steps,),
            in_specs=[weight_spec(d) for d in offsets]
            + [row_spec(k, columns) for k in range(streams) for _ in offsets]
            + [pl.BlockSpec((step_rows, features), lambda g, place_ref: (g, 0))]
            + [ANY] * len(after),
            out_specs=pl.BlockSpec((step_rows, features), lambda g, place_ref: (g, 0)),
            scratch_shapes=[pltpu.VMEM((count * columns, features), jnp.bfloat16)],
        ),
        out_shape=jax.ShapeDtypeStruct((streams * stream_rows, features), jnp.bfloat16),
        compiler_params=params(),
        cost_estimate=cost(),
        name="add_pieces",
    )(place, *([w_t] * count), *[p[d] for p in pieces for d in offsets], early, *after)


def ring(x, group, slot, job, w, a, b, dy):
    size = lax.axis_size("tensor")
    me = lax.axis_index("dp").astype(jnp.int32)
    blocks = group.shape[0]
    rows, features = x.shape
    length = rows // blocks
    columns = dy.shape[1]
    half = dy.shape[0] // 2
    cap = half // length
    streams = 2
    part_rows = rows // streams
    step_blocks = blocks // streams // 2
    group_rows = step_blocks * length

    order = [2 * r for r in range(size // 2)] + [2 * r + 1 for r in reversed(range(size // 2))]
    me_tensor = lax.axis_index("tensor").astype(jnp.int32)
    here = jnp.where(me_tensor % 2 == 0, me_tensor // 2, size - 1 - me_tensor // 2)
    there = (here + jnp.arange(size, dtype=jnp.int32)) % size
    place = jnp.where(there < size // 2, 2 * there, 2 * (size - 1 - there) + 1)
    ahead = [(order[r], order[(r + 1) % size]) for r in range(size)]
    back = [(order[r], order[(r - 1) % size]) for r in range(size)]
    swap = [(0, 1), (1, 0)]

    def right(v):
        return lax.ppermute(v, "tensor", ahead)

    def left(v):
        return lax.ppermute(v, "tensor", back)

    def exchange(v, bit):
        return lax.ppermute(v, "tensor", [(t, t ^ bit) for t in range(size)])

    mine = me[None]
    got = lax.ppermute(lax.dynamic_slice_in_dim(dy, (1 - me) * half, half), "dp", swap)

    far, near = size // 2, size // 2 - 1
    both = range(streams)
    ranks = a.shape[1]
    sums_r, sums_l, held_r, held_l, own, pieces = [], [], [], [], [], []

    def terms(k, offsets, received, plain, after):
        return project(
            x, k * part_rows, part_rows, w, place, offsets, received, plain, group_rows, columns, after
        )

    def first(k, after):
        r, l = terms(k, (far, size - near), (), False, after)
        sums_r.append(right(r))
        sums_l.append(left(l))
        return (r,)

    last = first(0, ())
    last = first(1, last)
    dy_home, *parts = home_gradient(dy, got, group, slot, mine, length, streams, last)
    for k in both:
        held_r.append(right(parts[k]))
        held_l.append(left(parts[k]))
        pieces.append({0: parts[k], size - 1: held_r[k], 1: held_l[k]})
    last = (dy_home,)
    low, coded = low_rank(x, a, dy_home, b.T, job, length, last)
    last = (coded,)
    bit = 1
    swapped = exchange(coded, bit)

    def low_step():
        nonlocal low, swapped, bit, last
        if bit >= size:
            return
        more = 2 * bit < size
        got = add_coded([(low, swapped)], length, last, True, more, low.shape[0] // length)
        low = got[0]
        last = (low,)
        bit *= 2
        if more:
            swapped = exchange(got[1], bit)

    w_t, a_t = w.T, a.T
    kept = sent = None
    for d in range(1, far):
        if d == far - 1:
            while bit < size:
                low_step()
            kept, sent = factor_gradients(
                x, dy_home, low, job, mine, ranks, length, last + (w_t, a_t)
            )
            last = (kept,)
        for k in both:
            if d == 2 and k == 0:
                last += (w_t, a_t)
            if near > d:
                turn_r, turn_l = terms(
                    k, (far - d, size - (near - d)), (sums_r[k], sums_l[k]), False, last
                )
                sums_l[k] = left(turn_l)
            else:
                turn_r, term = terms(k, (far - d, 0), (sums_r[k],), True, last)
                own.append(term)
            sums_r[k] = right(turn_r)
            last = (turn_r, held_l[k])
            if d < near:
                last += (held_r[k],)
                held_r[k] = right(held_r[k])
                pieces[k][size - 1 - d] = held_r[k]
            held_l[k] = left(held_l[k])
            pieces[k][1 + d] = held_l[k]
            if d + k == 2:
                low_step()

    grad_a, grad_b = add_factors(kept, lax.ppermute(sent, "dp", swap), features, last[:1])

    late = (far - 1, far)
    last = last[:1] + (pieces[0][far - 1],)
    early = None
    for k in both:
        ready = {d: v for d, v in pieces[k].items() if d not in late}
        early = input_gradient(
            ready, w_t, place, low, a_t, job, length, step_blocks // 2, k, early, last
        )
        last = (grad_b, pieces[1][far - 1])
    final = [{d: pieces[k][d] for d in late} for k in both]
    placed, sent = place_output(
        own, sums_r, sums_l, low, b, group, slot, job, mine, length, cap, (early,) + tuple(pieces[k][far] for k in both)
    )
    grad_home = add_pieces(final, early, w_t, place, 2, (placed,))
    output = complete(placed, lax.ppermute(sent, "dp", swap), mine)
    return output.reshape(dy.shape), grad_home, grad_a, grad_b


def local(*args):
    x, group, dy = args[0], args[1], args[7]
    size = lax.axis_size("tensor")
    blocks = group.shape[0]
    length = x.shape[0] // blocks
    fits = (
        lax.axis_size("dp") == 2
        and size % 2 == 0
        and size in (4, 8)
        and dy.shape[1] % 128 == 0
        and x.shape[1] % 128 == 0
        and length == LANES
        and args[5].shape[1] % (2 * LANES) == 0
        and blocks % 8 == 0
    )
    return ring(*args) if fits else general(*args)


def solution(mesh):
    return jax.shard_map(
        local,
        mesh=mesh,
        in_specs=(
            P(("parts", "dp"), "tensor"),
            P(("parts", "dp")),
            P(("parts", "dp")),
            P(("parts", "dp")),
            P("tensor", None),
            P("tensor", None),
            P(None, "tensor"),
            P(("parts", "dp"), "tensor"),
        ),
        out_specs=(
            P(("parts", "dp"), "tensor"),
            P(("parts", "dp"), "tensor"),
            P("tensor", ("parts", "dp")),
            P(("parts", "dp"), "tensor"),
        ),
        check_vma=False,
    )
```
